512 devices in a mesh: seq: 64 (over z_lo, x, core), batch: 8 (over z_hi, y).
Axes of the slice: x: 4, y: 4, z: 16 (z_hi: 2, z_lo: 8; z = z_hi * 8 + z_lo), core: 2. Of those that a mesh axis runs over, the one named last changes fastest.
Arguments:
- queries: bfloat16 [16, 4, 8192], P('batch'), may hold values from -45 to 45
- cache_levels: bfloat16 [16, 16384, 2048], P('batch', 'seq'), may hold values from -8 to 7, as said below
- scale_ids: int32 [16, 512], P('batch', 'seq'), may hold values from 0 to 15
- scale_table: float32 [16, 2048], P(None, 'batch'), may hold values from 0.05 to 0.5
- ctx_len: int32 [16, 64], P('batch', 'seq'), may hold values from 32 to 256, as said below
- span_rows: bfloat16 [16, 4096, 2048], P('batch', 'seq'), may hold values from -6 to 6
- span_len: int32 [16, 64], P('batch', 'seq'), may hold values from 16 to 64, as said below
- owners: int32 [16, 4096, 1], P('batch', 'seq'), may hold values from 0 to 63; in each aligned block of 64 rows (0 to 63, 64 to 127, ..., all dimensions but the last counted through in order) at most 2 rows name the same one
Outputs:
- attended: bfloat16 [16, 4, 8192], P('batch', None, 'seq')
- appended: bfloat16 [16, 8192, 2048], P('batch', 'seq')
The draws below stay inside these ranges and needn't reach their ends.
Inputs may be any that keep to these rules, and one draw needn't show every extreme that they name: `cache_levels`: integer levels. `ctx_len`: some request has all 256 rows valid on some index of seq. `span_len`: some request has all 64 rows valid on some index of seq. `owners`: within the 64 block rows of one device of one request no owner is named more than 2 times.
All inputs are finite; a program needn't handle non-finite values.
Results may differ from the reference program's by a relative error of at most 0.012.
The reference program's roundings to bfloat16 on the way count: a program that leaves them out, or rounds other values in their place, can miss the bound.
Values may be sent and summed in bfloat16 or wider, within the bound.
A program may use at most 128 MiB of HBM per device.

```python
import math
import jax
import jax.numpy as jnp
import numpy as np
from jax import lax

HQ = 64
KVH = 8
HD = 128
G = 8
STEPS = 4
SLOT = 256
SPAN_DEV = 64
CAP = 2
GROUP = 32
NSCALE = 16
REQUESTS = 16
CTX_MAX = 16384
SPAN_ROWS = 4096
APPEND_ROWS = 8192
N_SEQ = 64


def draw_queries(key, part):
    key = jax.random.fold_in(key, 11)
    first_key = jax.random.fold_in(key, 0)
    base = jnp.clip(jax.random.normal(first_key, (REQUESTS, STEPS, HQ, HD), jnp.float32), -6.0, 6.0)
    return base.reshape(REQUESTS, STEPS, HQ * HD).astype(jnp.bfloat16)


def draw_cache_levels(key, part):
    key = jax.random.fold_in(key, 12)
    levels = jax.random.randint(key, (REQUESTS, CTX_MAX, 2 * KVH * HD), -8, 8)
    return levels.astype(jnp.bfloat16)


def draw_ctx_len(key, part):
    key = jax.random.fold_in(key, 13)
    first_key, second_key = jax.random.split(key)
    lengths = jax.random.randint(first_key, (REQUESTS * N_SEQ,), SLOT // 8, SLOT + 1)
    chosen = jax.random.randint(second_key, (), 0, REQUESTS * N_SEQ)
    lengths = jnp.where(jnp.arange(REQUESTS * N_SEQ) == chosen, SLOT, lengths)
    return lengths.reshape(REQUESTS, N_SEQ).astype(jnp.int32)


def draw_span_len(key, part):
    key = jax.random.fold_in(key, 14)
    first_key, second_key = jax.random.split(key)
    lengths = jax.random.randint(first_key, (REQUESTS * N_SEQ,), SPAN_DEV // 4, SPAN_DEV + 1)
    chosen = jax.random.randint(second_key, (), 0, REQUESTS * N_SEQ)
    lengths = jnp.where(jnp.arange(REQUESTS * N_SEQ) == chosen, SPAN_DEV, lengths)
    return lengths.reshape(REQUESTS, N_SEQ).astype(jnp.int32)


def touch_ends(values, rng, smallest, largest):
    longest = values.shape.index(max(values.shape))
    spots = []
    for shift in (0, 1):
        where = [jax.random.randint(jax.random.fold_in(rng, axis), (), 0, length) for axis, length in enumerate(values.shape)]
        where[longest] = (where[longest] + shift) % values.shape[longest]
        spots.append(tuple(where))
    return values.at[spots[0]].set(smallest).at[spots[1]].set(largest)


def shard_levels(own_key, extent, shards, smallest, largest):
    factor_of, own = 1.0, jax.random.fold_in(own_key, 6)
    for axis_at, shards_of in shards:
        heights = jnp.exp(jax.random.uniform(jax.random.fold_in(own, axis_at), (shards_of,), jnp.float32, smallest / len(shards), largest / len(shards)))
        factor_of = factor_of * jnp.repeat(heights, extent[axis_at] // shards_of).reshape([-1 if axis == axis_at else 1 for axis in range(len(extent))])
    return factor_of


def routed_block(rng, own, number, rows, amount, top, most, lean):
    sequence = jax.random.permutation(rng, amount)
    heavy_load, ordinary = shares(amount, rows * top, most, lean, True), shares(amount, rows * top, most, lean, False)
    places = jnp.arange(amount)

    def named(sizes, offset_by):
        used = int((sizes > 0).sum())
        fixed = max(1, used // 4)
        moved = fixed + (places - fixed + offset_by * (used - fixed)) % max(1, amount - fixed)
        return jnp.zeros((amount,), jnp.int32).at[sequence[jnp.where(places < fixed, places, moved)]].set(jnp.asarray(sizes, jnp.int32))

    sizes = jnp.where(number % 4 == 0, named(heavy_load, number // 4), named(ordinary, number - number // 4 - 1))
    mixed = jax.random.permutation(jax.random.fold_in(own, 3), amount)
    source_of, taker = mixed[0:amount // 2 * 2:2], mixed[1:amount // 2 * 2:2]
    room = jnp.minimum(sizes[source_of] - 1, most - sizes[taker]) // 2
    room = jnp.where((source_of == sequence[0]) | (taker == sequence[0]) | (sizes[taker] == 0), 0, jnp.maximum(room, 0))
    moved = jax.random.randint(jax.random.fold_in(own, 4), (amount // 2,), 0, 1 << 20) % (room + 1)
    sizes = sizes.at[source_of].add(-moved).at[taker].add(moved)
    items = jnp.searchsorted(jnp.cumsum(sizes), jnp.arange(rows * top), side="right").astype(jnp.int32)
    grid = items.reshape(top, rows).T
    grid = grid[jax.random.permutation(jax.random.fold_in(own, 1), rows)]
    offset_by = jax.random.randint(jax.random.fold_in(own, 2), (rows, 1), 0, top)
    return jnp.take_along_axis(grid, (jnp.arange(top)[None, :] + offset_by) % top, axis=1)


def shares(number_of, total, reach, slope, full):
    weights = [(1 << 20) // math.isqrt(rank ** slope) + 1 for rank in range(1, number_of + 1)]
    largest = reach if full else min(reach, max(-(-total // number_of), total * weights[0] // sum(weights)))
    least = 1 if total - largest >= number_of - 1 else 0
    given, rest = [largest] + [least] * (number_of - 1), total - largest - least * (number_of - 1)
    while rest > 0:
        movable = [i for i in range(1, number_of) if given[i] < largest] or [i for i in range(1, number_of) if given[i] < reach]
        whole, left = sum([weights[i] for i in movable]), rest
        for i in movable:
            more = min(reach - given[i], max(1, left * weights[i] // whole), rest)
            given[i] = given[i] + more
            rest = rest - more
    return np.array(given)


def scatter_about(own_key, dims, spread, reach, cuts=(), kind=jnp.bfloat16):
    factor_of = shard_levels(own_key, dims, cuts, -0.22, 0.18) if cuts else 1.0
    values = jax.random.normal(own_key, dims, jnp.float32) * spread * factor_of
    return jnp.minimum(jnp.maximum(values, -reach), reach).astype(kind)


def setup_inputs(seed: int = 0) -> dict:
    seeds = jax.random.split(jax.random.key(seed), 9)
    queries = draw_queries(jax.random.fold_in(seeds[8], 71), 0)
    cache_levels = draw_cache_levels(jax.random.fold_in(seeds[8], 71), 0)
    scale_ids = touch_ends(jax.random.randint(seeds[2], (REQUESTS, CTX_MAX // GROUP), 0, NSCALE), jax.random.fold_in(seeds[2], 1), 0, NSCALE - 1).astype(jnp.int32)
    scale_table = jnp.clip(jnp.exp(math.log(0.5) - 2.3025851 * jax.random.uniform(seeds[3], (NSCALE, 2 * KVH * HD), jnp.float32) ** shard_levels(seeds[3], (NSCALE, 2 * KVH * HD), ((1, 8),), -0.2, 0.2)), 0.05, 0.5)
    ctx_len = draw_ctx_len(jax.random.fold_in(seeds[8], 71), 0)
    span_rows = scatter_about(seeds[5], (REQUESTS, SPAN_ROWS, 2 * KVH * HD), 1.0, 6.0, ((0, 8), (1, 64)))
    span_len = draw_span_len(jax.random.fold_in(seeds[8], 71), 0)
    owners_keys = jax.random.split(jax.random.fold_in(seeds[7], 1), REQUESTS * SPAN_ROWS // SPAN_DEV)
    owners_turns = jax.random.permutation(jax.random.fold_in(seeds[7], 3), REQUESTS * SPAN_ROWS // SPAN_DEV)
    owners = jax.vmap(lambda own, number: routed_block(jax.random.fold_in(seeds[7], 2), own, number, SPAN_DEV, N_SEQ, 1, CAP, 2))(owners_keys, owners_turns).reshape((REQUESTS, SPAN_ROWS, 1))
    return dict(queries=queries, cache_levels=cache_levels, scale_ids=scale_ids, scale_table=scale_table, ctx_len=ctx_len, span_rows=span_rows, span_len=span_len, owners=owners)


def hadamard(order):
    indices = jnp.arange(order, dtype=jnp.int32)
    common = jnp.bitwise_and(indices[:, None], indices[None, :])
    parity = jnp.zeros((order, order), jnp.int32)
    for bit_index in range(order.bit_length() - 1):
        parity = parity + jnp.bitwise_and(jnp.right_shift(common, bit_index), 1)
    signs = 1 - 2 * jnp.bitwise_and(parity, 1)
    return signs.astype(jnp.float32) / jnp.sqrt(jnp.float32(order))

def reference(queries, cache_levels, scale_ids, scale_table, ctx_len, span_rows, span_len, owners):
    row_width = 2 * KVH * HD
    rotate = hadamard(HD)
    span_local = jnp.arange(SPAN_ROWS, dtype=jnp.int32) % SPAN_DEV
    span_valid = span_local[None, :] < jnp.repeat(span_len, SPAN_DEV, axis=1, total_repeat_length=SPAN_ROWS)
    kept_rows = jnp.where(span_valid[..., None], span_rows, jnp.zeros_like(span_rows))
    cache_local = jnp.arange(CTX_MAX, dtype=jnp.int32) % SLOT
    cache_valid = cache_local[None, :] < jnp.repeat(ctx_len, SLOT, axis=1, total_repeat_length=CTX_MAX)

    def one_request(packed):
        query_row, levels, group_ids, context_valid, block_rows, block_valid = packed
        query_f32 = query_row.astype(jnp.float32).reshape(STEPS, HQ, HD)
        query_rot = jnp.einsum('shd,de->she', query_f32, rotate, precision=lax.Precision.HIGHEST).astype(jnp.bfloat16)
        scales = scale_table[group_ids]
        dequant = levels.astype(jnp.float32).reshape(CTX_MAX // GROUP, GROUP, row_width) * scales[:, None, :]
        dequant = dequant.reshape(CTX_MAX, row_width).astype(jnp.bfloat16)
        all_rows = jnp.concatenate([dequant, block_rows], axis=0)
        valid = jnp.concatenate([context_valid, block_valid])
        key_rows = all_rows[:, :KVH * HD].reshape(-1, KVH, HD).astype(jnp.float32)
        value_rows = all_rows[:, KVH * HD:].reshape(-1, KVH, HD).astype(jnp.float32)
        grouped = query_rot.reshape(STEPS, KVH, G, HD).astype(jnp.float32)
        scores = jnp.einsum('skgd,nkd->skgn', grouped, key_rows) / jnp.sqrt(jnp.float32(HD))
        masked = jnp.where(valid, scores, jnp.float32(-1e+30))
        row_max = lax.optimization_barrier(jnp.max(masked, axis=-1, keepdims=True))
        weights = jnp.where(valid, jnp.exp(masked - row_max), jnp.float32(0.0))
        weight_sum = lax.optimization_barrier(jnp.sum(weights, axis=-1))
        probs = weights.astype(jnp.bfloat16).astype(jnp.float32)
        accumulated = jnp.einsum('skgn,nkd->skgd', probs, value_rows)
        normed = accumulated / weight_sum[..., None]
        result = jnp.einsum('skgd,de->skge', normed, rotate, precision=lax.Precision.HIGHEST)
        return result.reshape(STEPS, HQ * HD).astype(jnp.bfloat16)
    attended = lax.map(one_request, (queries, cache_levels, scale_ids, cache_valid, kept_rows, span_valid))
    owner_ids = owners[..., 0]
    onehot = (owner_ids[..., None] == jnp.arange(N_SEQ, dtype=jnp.int32)).astype(jnp.int32)
    onehot = onehot.reshape(REQUESTS, N_SEQ, SPAN_DEV, N_SEQ)
    before = jnp.cumsum(onehot, axis=2) - onehot
    slot_rank = lax.optimization_barrier(jnp.sum(before * onehot, axis=-1)).reshape(REQUESTS, SPAN_ROWS)
    source = jnp.arange(SPAN_ROWS, dtype=jnp.int32) // SPAN_DEV
    target = owner_ids * (N_SEQ * CAP) + source[None, :] * CAP + slot_rank
    appended = jnp.zeros((REQUESTS, APPEND_ROWS, row_width), jnp.bfloat16)
    request_index = jnp.arange(REQUESTS, dtype=jnp.int32)[:, None]
    appended = appended.at[request_index, target.astype(jnp.int32)].set(kept_rows)
    return (attended, appended)
```

```python
import functools

import jax
import jax.numpy as jnp
from jax import lax
from jax.experimental import pallas as pl
from jax.experimental.pallas import tpu as pltpu
from jax.sharding import PartitionSpec as P

HQ = 64
KVH = 8
HD = 128
G = 8
CAP = 2
GROUP = 32
NSCALE = 16
STEPS = 4
SLOT = 256
SPAN = 64
REQ = 2
WIDTH = 2 * KVH * HD
SEQ = 64
PLANE = 8
LAYERS = 8
BATCH_Y = 4
PIECE = WIDTH // 4
MESH = pl.DeviceIdType.MESH
F32 = jnp.float32
BF16 = jnp.bfloat16


def iota(shape, axis):
    return lax.broadcasted_iota(jnp.int32, shape, axis)


def hadamard_signs():
    common = jnp.bitwise_and(iota((HD, HD), 0), iota((HD, HD), 1))
    parity = jnp.zeros((HD, HD), jnp.int32)
    for bit in range(7):
        parity = parity + jnp.bitwise_and(jnp.right_shift(common, bit), 1)
    return (1 - 2 * jnp.bitwise_and(parity, 1)).astype(F32).astype(BF16)


def dot(a, b, contract=((1,), (0,))):
    return lax.dot_general(a, b, (contract, ((), ())), preferred_element_type=F32)


def exchange_kernel(
    q_ref, lev_hbm, ids_ref, tab_ref, ctx_ref, span_hbm, slen_ref, own_ref,
    land_hbm, part_hbm,
    lev, span, send, tbl, scales, qrot, mask, first_out, first_in, second_out,
    lev_sem, span_sem, own_sem, part_sem,
    a2a_send, a2a_recv, zh_send, zh_recv, y_send, y_recv,
    first_send, first_recv, second_send, second_recv,
):
    me = lax.axis_index("seq")
    layer, place = me // PLANE, lax.rem(me, PLANE)
    batch = lax.axis_index("batch")
    far, row = batch // BATCH_Y, lax.rem(batch, BATCH_Y)

    barrier = pltpu.get_barrier_semaphore()

    def greet(i, carry):
        pl.semaphore_signal(
            barrier, inc=1, device_id={"seq": lax.rem(me + i, SEQ)}, device_id_type=MESH
        )
        return carry

    lax.fori_loop(1, SEQ, greet, 0)
    partner = lax.rem(batch + BATCH_Y, 2 * BATCH_Y)
    pl.semaphore_signal(barrier, inc=1, device_id={"batch": partner}, device_id_type=MESH)
    sides = [far * BATCH_Y + lax.rem(row + i, BATCH_Y) for i in range(1, BATCH_Y)]
    for side in sides:
        pl.semaphore_signal(barrier, inc=1, device_id={"batch": side}, device_id_type=MESH)

    span_copy = pltpu.make_async_copy(span_hbm, span, span_sem)
    span_copy.start()
    lev_copy = pltpu.make_async_copy(lev_hbm, lev, lev_sem)
    lev_copy.start()

    owner_col = jnp.concatenate([own_ref[0], own_ref[1]], axis=0).astype(F32)
    above, along = iota((2 * SPAN, 2 * SPAN), 0), iota((2 * SPAN, 2 * SPAN), 1)
    owner_wide = jnp.broadcast_to(owner_col, (2 * SPAN, 2 * SPAN))
    owner_row = jnp.sum(jnp.where(above == along, owner_wide, 0.0), axis=0, keepdims=True)
    same = (owner_wide == owner_row) & (above < along) & (above // SPAN == along // SPAN)
    rank = jnp.sum(jnp.where(same, 1.0, 0.0), axis=0, keepdims=True)
    lane = iota((1, 2 * SPAN), 1)
    request = lane // SPAN
    kept = lax.rem(lane, SPAN) < jnp.where(request == 0, slen_ref[0, 0], slen_ref[1, 0])
    target = owner_row.astype(jnp.int32) * 16 + request * 8 + rank.astype(jnp.int32)
    target = jnp.concatenate(
        [jnp.where(kept, target + 2 * quarter, -1) for quarter in range(4)], axis=1
    )
    span_copy.wait()
    stacked = jnp.concatenate(
        [
            span[r, :, quarter * PIECE : (quarter + 1) * PIECE]
            for quarter in range(4)
            for r in range(REQ)
        ],
        axis=0,
    )
    for chunk in range(4):
        rows = iota((256, 512), 0) + chunk * 256
        pick = jnp.where(rows == target, 1.0, 0.0).astype(BF16)
        block = dot(pick, stacked).astype(BF16)
        send[chunk * 16 : (chunk + 1) * 16] = block.reshape(16, 16, PIECE)

    signs = hadamard_signs()
    root = jnp.float32(1.0) / jnp.sqrt(jnp.float32(HD))
    queries = jnp.concatenate([q_ref[0].astype(F32), q_ref[1].astype(F32)], axis=0)
    stacked_q = jnp.concatenate(
        [queries[:, h * HD : (h + 1) * HD] for h in range(HQ)], axis=0
    ).astype(BF16)
    qrot[...] = (dot(stacked_q, signs) * root).astype(BF16)

    keys = REQ * (SLOT + SPAN)
    wanted = lax.rem(iota((64, keys), 0) // STEPS, REQ)
    column = iota((64, keys), 1)
    in_slot = column < REQ * SLOT
    other = column - REQ * SLOT
    key_request = jnp.where(in_slot, column // SLOT, other // SPAN)
    position = jnp.where(in_slot, lax.rem(column, SLOT), lax.rem(other, SPAN))
    first = key_request == 0
    limit = jnp.where(
        in_slot,
        jnp.where(first, ctx_ref[0, 0], ctx_ref[1, 0]),
        jnp.where(first, slen_ref[0, 0], slen_ref[1, 0]),
    )
    mask[...] = jnp.where((wanted == key_request) & (position < limit), 1.0, 0.0)
    blocks = REQ * (SLOT // GROUP)
    group = jnp.zeros((blocks, 3 * NSCALE), jnp.int32)
    for r in range(REQ):
        for b in range(SLOT // GROUP):
            here = iota((blocks, 3 * NSCALE), 0) == r * (SLOT // GROUP) + b
            group = jnp.where(here, ids_ref[r, b], group)
    chosen = jnp.where(lax.rem(iota((blocks, 3 * NSCALE), 1), NSCALE) == group, 1.0, 0.0).astype(BF16)
    tbl[row, far] = tab_ref[...]

    pl.semaphore_wait(barrier, SEQ - 1 + BATCH_Y)

    far_copy = pltpu.make_async_remote_copy(
        src_ref=tbl.at[row, far], dst_ref=tbl.at[row, far], send_sem=zh_send, recv_sem=zh_recv,
        device_id={"batch": partner}, device_id_type=MESH,
    )
    far_copy.start()

    keep = pltpu.make_async_copy(send.at[me], land_hbm.at[me], own_sem)
    keep.start()

    def post(i, carry):
        step = i // PLANE
        to_layer = jnp.where(layer < LAYERS // 2, LAYERS - 1 - step, step)
        to = to_layer * PLANE + lax.rem(place + lax.rem(i, PLANE), PLANE)

        @pl.when(to != me)
        def _():
            pltpu.make_async_remote_copy(
                src_ref=send.at[to], dst_ref=land_hbm.at[me], send_sem=a2a_send, recv_sem=a2a_recv,
                device_id={"seq": to}, device_id_type=MESH,
            ).start()

        return carry

    lax.fori_loop(0, SEQ, post, 0)

    far_copy.wait()
    side_copies = [
        pltpu.make_async_remote_copy(
            src_ref=tbl.at[row], dst_ref=tbl.at[row], send_sem=y_send, recv_sem=y_recv,
            device_id={"batch": side}, device_id_type=MESH,
        )
        for side in sides
    ]
    for copy in side_copies:
        copy.start()
    lev_copy.wait()
    sides_all = pltpu.make_async_remote_copy(
        src_ref=tbl.at[pl.ds(0, BATCH_Y - 1)], dst_ref=tbl.at[pl.ds(0, BATCH_Y - 1)],
        send_sem=y_send, recv_sem=y_recv, device_id={"batch": partner}, device_id_type=MESH,
    )
    sides_all.wait_send()
    sides_all.wait_recv()

    for r in range(BATCH_Y):
        for f in range(2):
            piece = tbl[r, f]
            high = piece.astype(BF16)
            rest = piece - high.astype(F32)
            middle = rest.astype(BF16)
            low = (rest - middle.astype(F32)).astype(BF16)
            scales[r, f] = dot(chosen, jnp.concatenate([high, middle, low], axis=0))

    lane_stat = iota((64, HD), 1) < HD // 2

    def dequant(pair, half, base, part):
        pieces = []
        lanes = pl.ds(pl.multiple_of(base, HD), HD)
        for r in range(REQ):
            for b in range(SLOT // GROUP):
                at = r * (SLOT // GROUP) + b
                scale = scales[pair, part, at : at + 1, half * HD : (half + 1) * HD]
                level = lev[r, b * GROUP : (b + 1) * GROUP, lanes].astype(F32)
                pieces.append((level * scale).astype(BF16))
        for r in range(REQ):
            pieces.append(span[r, :, lanes])
        return jnp.concatenate(pieces, axis=0)

    def head_pair(pair, carry):
        for half in range(2):
            head = pair * 2 + half
            key_rows = dequant(pair, half, head * HD, 0)
            q = qrot[pl.ds(pl.multiple_of(head * 64, 64), 64), :]
            scores = dot(q, key_rows, ((1,), (1,))) * root
            scores = jnp.where(mask[...] > 0.0, scores, jnp.float32(-1e30))
            top = jnp.max(scores, axis=1, keepdims=True)
            weights = jnp.exp(scores - top)
            total = jnp.sum(weights, axis=1, keepdims=True)
            value_rows = dequant(pair, half, (KVH + head) * HD, 1)
            acc = dot(weights.astype(BF16), value_rows)
            stat = jnp.where(
                lane_stat, jnp.broadcast_to(top, (64, HD)), jnp.broadcast_to(total, (64, HD))
            )
            at = pl.ds(pl.multiple_of(head * 8, 8), 8)
            for g in range(G):
                first_out[g, 0, at, :] = acc[g * 8 : (g + 1) * 8]
                first_out[g, 1, at, :] = stat[g * 8 : (g + 1) * 8]
        return carry

    lax.fori_loop(0, KVH // 2, head_pair, 0)

    def first_post(i, carry):
        to = lax.rem(place + i, PLANE)
        pltpu.make_async_remote_copy(
            src_ref=first_out.at[to], dst_ref=first_in.at[place],
            send_sem=first_send, recv_sem=first_recv,
            device_id={"seq": layer * PLANE + to}, device_id_type=MESH,
        ).start()
        return carry

    lax.fori_loop(1, PLANE, first_post, 0)
    first_in[place] = first_out[place]
    first_all = pltpu.make_async_remote_copy(
        src_ref=first_out.at[pl.ds(0, PLANE - 1)], dst_ref=first_in.at[pl.ds(0, PLANE - 1)],
        send_sem=first_send, recv_sem=first_recv, device_id={"seq": me}, device_id_type=MESH,
    )
    first_all.wait_send()
    first_all.wait_recv()
    acc, stat = combine([(first_in[i, 0], first_in[i, 1]) for i in range(PLANE)])
    second_out[:, 0] = acc.reshape(LAYERS, 8, HD)
    second_out[:, 1] = stat.reshape(LAYERS, 8, HD)

    def second_post(i, carry):
        to = lax.rem(layer + i, LAYERS)
        pltpu.make_async_remote_copy(
            src_ref=second_out.at[to], dst_ref=part_hbm.at[layer],
            send_sem=second_send, recv_sem=second_recv,
            device_id={"seq": to * PLANE + place}, device_id_type=MESH,
        ).start()
        return carry

    lax.fori_loop(1, LAYERS, second_post, 0)
    own_part = pltpu.make_async_copy(second_out.at[layer], part_hbm.at[layer], part_sem)
    own_part.start()
    own_part.wait()
    second_all = pltpu.make_async_remote_copy(
        src_ref=second_out.at[pl.ds(0, LAYERS - 1)], dst_ref=part_hbm.at[pl.ds(0, LAYERS - 1)],
        send_sem=second_send, recv_sem=second_recv, device_id={"seq": me}, device_id_type=MESH,
    )
    second_all.wait_send()
    second_all.wait_recv()

    keep.wait()
    rows_all = pltpu.make_async_remote_copy(
        src_ref=send.at[pl.ds(0, SEQ - 1)], dst_ref=land_hbm.at[pl.ds(0, SEQ - 1)],
        send_sem=a2a_send, recv_sem=a2a_recv, device_id={"seq": me}, device_id_type=MESH,
    )
    rows_all.wait_send()
    rows_all.wait_recv()


def combine(parts):
    tops = [stat[:, 0:1] for _, stat in parts]
    top = functools.reduce(jnp.maximum, tops)
    acc = total = None
    for (values, stat), own_top in zip(parts, tops):
        factor = jnp.exp(own_top - top)
        scaled, weight = values * factor, stat[:, HD // 2 : HD // 2 + 1] * factor
        acc = scaled if acc is None else acc + scaled
        total = weight if total is None else total + weight
    shape = acc.shape
    left = iota(shape, 1) < HD // 2
    return acc, jnp.where(left, jnp.broadcast_to(top, shape), jnp.broadcast_to(total, shape))


def finish_kernel(land_hbm, part_ref, att_ref, app_hbm, land, app, in_sems, out_sems):
    chunks = SEQ // 8
    for c in range(chunks):
        pltpu.make_async_copy(
            land_hbm.at[pl.ds(c * 8, 8)], land.at[pl.ds(c * 8, 8)], in_sems.at[c]
        ).start()
    to = iota((128, 128), 0)
    request, quarter = to // 64, lax.rem(to // 16, 4)
    source, rank = lax.rem(to // 2, 8), lax.rem(to, 2)
    wanted = source * 16 + request * 8 + quarter * 2 + rank
    move = jnp.where(iota((128, 128), 1) == wanted, 1.0, 0.0).astype(BF16)

    acc, stat = combine([(part_ref[i, 0], part_ref[i, 1]) for i in range(LAYERS)])
    normed = acc / stat[:, HD // 2 : HD // 2 + 1]
    signs = hadamard_signs()
    high = normed.astype(BF16)
    rest = normed - high.astype(F32)
    middle = rest.astype(BF16)
    low = (rest - middle.astype(F32)).astype(BF16)
    root = jnp.float32(1.0) / jnp.sqrt(jnp.float32(HD))
    turned = (dot(low, signs) + dot(middle, signs) + dot(high, signs)) * root
    att_ref[0] = turned[0:STEPS].astype(BF16)
    att_ref[1] = turned[STEPS : 2 * STEPS].astype(BF16)

    def out_copy(c):
        rows = pl.ds(c * 16, 16)
        return pltpu.make_async_copy(app.at[:, rows, :], app_hbm.at[:, rows, :], out_sems.at[c])

    for c in range(chunks):
        pltpu.make_async_copy(
            land_hbm.at[pl.ds(c * 8, 8)], land.at[pl.ds(c * 8, 8)], in_sems.at[c]
        ).wait()
        block = land[c * 8 : (c + 1) * 8].reshape(128, PIECE)
        moved = dot(move, block).astype(BF16)
        for r in range(REQ):
            for q in range(4):
                start = r * 64 + q * 16
                app[r, c * 16 : (c + 1) * 16, q * PIECE : (q + 1) * PIECE] = moved[start : start + 16]
        out_copy(c).start()
    for c in range(chunks):
        out_copy(c).wait()


def local(queries, cache_levels, scale_ids, scale_table, ctx_len, span_rows, span_len, owners):
    vmem, smem = pl.BlockSpec(memory_space=pltpu.VMEM), pl.BlockSpec(memory_space=pltpu.SMEM)
    anywhere = pl.BlockSpec(memory_space=pl.ANY)
    dma = pltpu.SemaphoreType.DMA
    landed, parts = pl.pallas_call(
        exchange_kernel,
        out_shape=(
            jax.ShapeDtypeStruct((SEQ, 16, PIECE), BF16),
            jax.ShapeDtypeStruct((LAYERS, 2, 8, HD), F32),
        ),
        in_specs=[vmem, anywhere, smem, vmem, smem, anywhere, smem, vmem],
        out_specs=(anywhere, anywhere),
        scratch_shapes=[
            pltpu.VMEM((REQ, SLOT, WIDTH), BF16),
            pltpu.VMEM((REQ, SPAN, WIDTH), BF16),
            pltpu.VMEM((SEQ, 16, PIECE), BF16),
            pltpu.VMEM((BATCH_Y, 2, NSCALE, 256), F32),
            pltpu.VMEM((BATCH_Y, 2, REQ * (SLOT // GROUP), 256), F32),
            pltpu.VMEM((HQ * 8, HD), BF16),
            pltpu.VMEM((64, REQ * (SLOT + SPAN)), F32),
            pltpu.VMEM((PLANE, 2, 64, HD), F32),
            pltpu.VMEM((PLANE, 2, 64, HD), F32),
            pltpu.VMEM((LAYERS, 2, 8, HD), F32),
        ]
        + [dma] * 14,
        compiler_params=pltpu.CompilerParams(
            collective_id=0, has_side_effects=True, vmem_limit_bytes=40 * 2**20
        ),
        cost_estimate=pl.CostEstimate(
            flops=2 * 10**9, bytes_accessed=5 * 2**20, transcendentals=400000
        ),
        name="exchange",
    )(queries, cache_levels, scale_ids, scale_table, ctx_len, span_rows, span_len, owners)
    return pl.pallas_call(
        finish_kernel,
        out_shape=(
            jax.ShapeDtypeStruct((REQ, STEPS, HD), BF16),
            jax.ShapeDtypeStruct((REQ, SEQ * CAP, WIDTH), BF16),
        ),
        in_specs=[anywhere, vmem],
        out_specs=(vmem, anywhere),
        scratch_shapes=[
            pltpu.VMEM((SEQ, 16, PIECE), BF16),
            pltpu.VMEM((REQ, SEQ * CAP, WIDTH), BF16),
            dma((8,)),
            dma((8,)),
        ],
        compiler_params=pltpu.CompilerParams(vmem_limit_bytes=40 * 2**20),
        name="finish",
    )(landed, parts)


def solution(mesh):
    return jax.shard_map(
        local,
        mesh=mesh,
        in_specs=(
            P("batch", None, None),
            P("batch", "seq", None),
            P("batch", "seq"),
            P(None, "batch"),
            P("batch", "seq"),
            P("batch", "seq", None),
            P("batch", "seq"),
            P("batch", "seq", None),
        ),
        out_specs=(P("batch", None, "seq"), P("batch", "seq", None)),
        check_vma=False,
    )
```

```python
import functools

import jax
import jax.numpy as jnp
from jax import lax
from jax.experimental import pallas as pl
from jax.experimental.pallas import tpu as pltpu
from jax.sharding import PartitionSpec as P

HQ = 64
KVH = 8
HD = 128
G = 8
CAP = 2
GROUP = 32
NSCALE = 16
STEPS = 4
SLOT = 256
SPAN = 64
REQ = 2
WIDTH = 2 * KVH * HD
SEQ = 64
PLANE = 8
LAYERS = 8
BATCH_Y = 4
PIECE = WIDTH // 4
VMEM = 60 * 2**20
MESH = pl.DeviceIdType.MESH
F32 = jnp.float32
BF16 = jnp.bfloat16


def iota(shape, axis):
    return lax.broadcasted_iota(jnp.int32, shape, axis)


def hadamard_signs():
    common = jnp.bitwise_and(iota((HD, HD), 0), iota((HD, HD), 1))
    parity = jnp.zeros((HD, HD), jnp.int32)
    for bit in range(7):
        parity = parity + jnp.bitwise_and(jnp.right_shift(common, bit), 1)
    return (1 - 2 * jnp.bitwise_and(parity, 1)).astype(F32).astype(BF16)


def dot(a, b, contract=((1,), (0,))):
    return lax.dot_general(a, b, (contract, ((), ())), preferred_element_type=F32)


def as_column(row, hot):
    return jnp.sum(jnp.where(hot, jnp.broadcast_to(row, hot.shape), 0.0), axis=1, keepdims=True)


def join(stats):
    tops = jnp.concatenate([stat[0:1] for stat in stats], axis=0)
    totals = jnp.concatenate([stat[1:2] for stat in stats], axis=0)
    top = jnp.max(tops, axis=0, keepdims=True)
    factors = jnp.exp(tops - top)
    return factors, top, jnp.sum(totals * factors, axis=0, keepdims=True)


def exchange_kernel(
    q_hbm, lev_hbm, ids_ref, tab_hbm, ctx_ref, span_hbm, slen_ref, own_ref,
    land_hbm, att_ref,
    q_ref, lev, span, send, tbl, scales, qrot, mask,
    first_out, first_in, first_stat, first_got, second_out, second_in, second_stat, second_got,
    q_sem, tab_sem, lev_sem, span_sem, own_sem,
    a2a_send, a2a_recv, far_send, far_recv, near_send, near_recv, side_send, side_recv,
    first_send, first_recv, first_stat_send, first_stat_recv,
    second_send, second_recv, second_stat_send, second_stat_recv,
    ready,
):
    me = lax.axis_index("seq")
    layer, place = me // PLANE, lax.rem(me, PLANE)
    batch = lax.axis_index("batch")
    far, row = batch // BATCH_Y, lax.rem(batch, BATCH_Y)
    partner = lax.rem(batch + BATCH_Y, 2 * BATCH_Y)
    sides = [far * BATCH_Y + lax.rem(row + i, BATCH_Y) for i in range(1, BATCH_Y)]
    lower = layer < LAYERS // 2

    def loop(start, stop, body):
        def step(i, carry):
            body(i)
            return carry

        lax.fori_loop(start, stop, step, 0)

    barrier = pltpu.get_barrier_semaphore()

    def greet(to):
        pl.semaphore_signal(barrier, inc=1, device_id=to, device_id_type=MESH)

    loop(1, PLANE, lambda i: greet({"seq": layer * PLANE + lax.rem(place + i, PLANE)}))
    for side in sides:
        greet({"batch": side})
    pl.when(far == 0)(lambda: greet({"batch": partner}))
    loop((layer + 1) * PLANE, SEQ, lambda i: greet({"seq": i}))

    span_copy = pltpu.make_async_copy(span_hbm, span, span_sem)
    span_copy.start()
    tab_copy = pltpu.make_async_copy(tab_hbm, tbl.at[far, row], tab_sem)
    tab_copy.start()
    q_copy = pltpu.make_async_copy(q_hbm, q_ref, q_sem)
    q_copy.start()
    lev_copy = pltpu.make_async_copy(lev_hbm, lev, lev_sem)
    lev_copy.start()

    owner_row = jnp.concatenate([own_ref[0], own_ref[1]], axis=1).astype(F32)
    above, along = iota((2 * SPAN, 2 * SPAN), 0), iota((2 * SPAN, 2 * SPAN), 1)
    owner_wide = jnp.broadcast_to(owner_row, (2 * SPAN, 2 * SPAN))
    owner_col = jnp.sum(jnp.where(above == along, owner_wide, 0.0), axis=1, keepdims=True)
    same = (owner_wide == owner_col) & (above < along) & (above // SPAN == along // SPAN)
    rank = jnp.sum(jnp.where(same, 1.0, 0.0), axis=0, keepdims=True)
    lane = iota((1, 2 * SPAN), 1)
    request = lane // SPAN
    kept = lax.rem(lane, SPAN) < jnp.where(request == 0, slen_ref[0, 0], slen_ref[0, 1])
    target = owner_row.astype(jnp.int32) * 16 + request * 8 + rank.astype(jnp.int32)
    target = jnp.concatenate(
        [jnp.where(kept, target + 2 * quarter, -1) for quarter in range(4)], axis=1
    )
    span_copy.wait()
    stacked = jnp.concatenate(
        [
            span[r, :, quarter * PIECE : (quarter + 1) * PIECE]
            for quarter in range(4)
            for r in range(REQ)
        ],
        axis=0,
    )
    for to_layer in range(LAYERS):
        rows = iota((16 * PLANE, REQ * SPAN * 4), 0) + to_layer * (16 * PLANE)
        pick = jnp.where(rows == target, 1.0, 0.0).astype(BF16)
        block = dot(pick, stacked).astype(BF16)
        send[pl.ds(to_layer * PLANE, PLANE)] = block.reshape(PLANE, 16, PIECE)

    pl.semaphore_wait(barrier, PLANE - 1 + BATCH_Y - 1 + far + layer * PLANE)

    loop(
        0,
        layer,
        lambda i: pl.semaphore_signal(
            ready.at[layer], inc=1, device_id={"seq": i * PLANE + place}, device_id_type=MESH
        ),
    )

    tab_copy.wait()
    far_copy = pltpu.make_async_remote_copy(
        src_ref=tbl.at[far, row], dst_ref=tbl.at[far, row], send_sem=far_send, recv_sem=far_recv,
        device_id={"batch": partner}, device_id_type=MESH,
    )
    pl.when(far == 1)(far_copy.start)

    def to_sides(half, send_sem, recv_sem):
        for side in sides:
            pltpu.make_async_remote_copy(
                src_ref=tbl.at[half, row], dst_ref=tbl.at[half, row],
                send_sem=send_sem, recv_sem=recv_sem,
                device_id={"batch": side}, device_id_type=MESH,
            ).start()

    def from_sides(send_sem, recv_sem):
        some = tbl.at[0, pl.ds(0, BATCH_Y - 1)]
        every = pltpu.make_async_remote_copy(
            src_ref=some, dst_ref=some, send_sem=send_sem, recv_sem=recv_sem,
            device_id={"batch": partner}, device_id_type=MESH,
        )
        every.wait_send()
        every.wait_recv()

    to_sides(far, near_send, near_recv)

    def await_layer(to_layer):
        pl.when(to_layer > layer)(lambda: pl.semaphore_wait(ready.at[to_layer], 1))

    def send_rows(to_layer, start=0):
        def one(i):
            to = to_layer * PLANE + lax.rem(place + i, PLANE)
            pltpu.make_async_remote_copy(
                src_ref=send.at[to], dst_ref=land_hbm.at[me], send_sem=a2a_send, recv_sem=a2a_recv,
                device_id={"seq": to}, device_id_type=MESH,
            ).start()

        loop(start, PLANE, one)

    def post(to_layer):
        await_layer(to_layer)
        send_rows(to_layer)

    half = LAYERS // 2
    base = layer // half * half
    across = [jnp.where(lower, half + i, half - 1 - i) for i in (0, 3, 1, 2)]
    beside = [base + lax.rem(layer + i, half) for i in range(1, half)]

    rest = [across[2], beside[0], beside[1], across[3], beside[2]]
    post(across[0])
    post(across[1])
    send_rows(layer, 1)
    keep = pltpu.make_async_copy(send.at[me], land_hbm.at[me], own_sem)
    keep.start()

    @pl.when(far == 1)
    def _():
        for to_layer in rest[: 5]:
            post(to_layer)

    signs = hadamard_signs()
    root = jnp.float32(1.0) / jnp.sqrt(jnp.float32(HD))
    q_copy.wait()
    queries = jnp.concatenate([q_ref[0].astype(F32), q_ref[1].astype(F32)], axis=0)
    stacked_q = jnp.concatenate(
        [queries[:, h * HD : (h + 1) * HD] for h in range(HQ)], axis=0
    ).astype(BF16)
    qrot[...] = (dot(stacked_q, signs) * root).astype(BF16)

    keys = REQ * (SLOT + SPAN)
    wanted = lax.rem(iota((64, keys), 0) // STEPS, REQ)
    column = iota((64, keys), 1)
    in_slot = column < REQ * SLOT
    other = column - REQ * SLOT
    key_request = jnp.where(in_slot, column // SLOT, other // SPAN)
    position = jnp.where(in_slot, lax.rem(column, SLOT), lax.rem(other, SPAN))
    first = key_request == 0
    limit = jnp.where(
        in_slot,
        jnp.where(first, ctx_ref[0, 0], ctx_ref[0, 1]),
        jnp.where(first, slen_ref[0, 0], slen_ref[0, 1]),
    )
    mask[...] = jnp.where((wanted == key_request) & (position < limit), 1.0, 0.0)
    blocks = REQ * (SLOT // GROUP)
    group = jnp.zeros((blocks, 3 * NSCALE), jnp.int32)
    for r in range(REQ):
        for b in range(SLOT // GROUP):
            here = iota((blocks, 3 * NSCALE), 0) == r * (SLOT // GROUP) + b
            group = jnp.where(here, ids_ref[r, b], group)
    chosen = jnp.where(lax.rem(iota((blocks, 3 * NSCALE), 1), NSCALE) == group, 1.0, 0.0).astype(BF16)

    far_copy.wait_recv()

    @pl.when(far == 0)
    def _():
        far_copy.start()
        for to_layer in rest[: 3]:
            post(to_layer)

    to_sides(1 - far, side_send, side_recv)
    from_sides(near_send, near_recv)
    from_sides(side_send, side_recv)

    for f in range(2):
        for r in range(BATCH_Y):
            piece = tbl[f, r]
            high = piece.astype(BF16)
            remain = piece - high.astype(F32)
            middle = remain.astype(BF16)
            low = (remain - middle.astype(F32)).astype(BF16)
            scales[f, r] = dot(chosen, jnp.concatenate([high, middle, low], axis=0))
    lev_copy.wait()

    lane = iota((64, HD), 1)
    sub = lax.rem(iota((64, HD), 0), 8)

    def dequant(pair, half, base, part):
        pieces = []
        lanes = pl.ds(pl.multiple_of(base, HD), HD)
        for r in range(REQ):
            for b in range(SLOT // GROUP):
                at = r * (SLOT // GROUP) + b
                scale = scales[part, pair, at : at + 1, half * HD : (half + 1) * HD]
                level = lev[r, b * GROUP : (b + 1) * GROUP, lanes].astype(F32)
                pieces.append((level * scale).astype(BF16))
        for r in range(REQ):
            pieces.append(span[r, :, lanes])
        return jnp.concatenate(pieces, axis=0)

    def head_pair(pair, carry):
        tops, totals = carry
        for half in range(2):
            head = pair * 2 + half
            key_rows = dequant(pair, half, head * HD, 0)
            q = qrot[pl.ds(pl.multiple_of(head * 64, 64), 64), :]
            scores = dot(q, key_rows, ((1,), (1,))) * root
            scores = jnp.where(mask[...] > 0.0, scores, jnp.float32(-1e30))
            top = jnp.max(scores, axis=1, keepdims=True)
            weights = jnp.exp(scores - top)
            total = jnp.sum(weights, axis=1, keepdims=True)
            value_rows = dequant(pair, half, (KVH + head) * HD, 1)
            acc = dot(weights.astype(BF16), value_rows)
            hot = lane == head * 8 + sub
            tops = tops + jnp.sum(jnp.where(hot, top, 0.0).reshape(G, 8, HD), axis=1)
            totals = totals + jnp.sum(jnp.where(hot, total, 0.0).reshape(G, 8, HD), axis=1)
            at = pl.ds(pl.multiple_of(head * 8, 8), 8)
            for g in range(G):
                first_out[g, at, :] = acc[g * 8 : (g + 1) * 8]
        return tops, totals

    zeros = jnp.zeros((G, HD), F32)
    tops, totals = lax.fori_loop(0, KVH // 2, head_pair, (zeros, zeros))
    for g in range(G):
        first_stat[g, 0:1] = tops[g : g + 1]
        first_stat[g, 1:2] = totals[g : g + 1]

    def first_post(i):
        to = lax.rem(place + i, PLANE)
        for out, into, send_sem, recv_sem in (
            (first_out, first_in, first_send, first_recv),
            (first_stat, first_got, first_stat_send, first_stat_recv),
        ):
            pltpu.make_async_remote_copy(
                src_ref=out.at[to], dst_ref=into.at[place], send_sem=send_sem, recv_sem=recv_sem,
                device_id={"seq": layer * PLANE + to}, device_id_type=MESH,
            ).start()

    def wait_all(out, into, count, send_sem, recv_sem):
        every = pltpu.make_async_remote_copy(
            src_ref=out.at[pl.ds(0, count)], dst_ref=into.at[pl.ds(0, count)],
            send_sem=send_sem, recv_sem=recv_sem, device_id={"seq": me}, device_id_type=MESH,
        )
        every.wait_send()
        every.wait_recv()

    loop(1, PLANE, first_post)
    first_in[place] = first_out[place]
    first_got[place] = first_stat[place]
    wait_all(first_out, first_in, PLANE - 1, first_send, first_recv)
    wait_all(first_stat, first_got, PLANE - 1, first_stat_send, first_stat_recv)
    factors, top, total = join([first_got[i] for i in range(PLANE)])
    hot = lane == iota((64, HD), 0)
    acc = None
    for i in range(PLANE):
        term = first_in[i] * as_column(factors[i : i + 1], hot)
        acc = term if acc is None else acc + term
    second_out[...] = acc.reshape(LAYERS, 8, HD)
    second_stat[0, 0:1] = top
    second_stat[0, 1:2] = total

    def second_post(i):
        to = lax.rem(layer + i, LAYERS)
        for out, into, send_sem, recv_sem in (
            (second_out.at[to], second_in, second_send, second_recv),
            (second_stat.at[0], second_got, second_stat_send, second_stat_recv),
        ):
            pltpu.make_async_remote_copy(
                src_ref=out, dst_ref=into.at[layer], send_sem=send_sem, recv_sem=recv_sem,
                device_id={"seq": to * PLANE + place}, device_id_type=MESH,
            ).start()

    @pl.when(far == 0)
    def _():
        for to_layer in rest[3 :]:
            await_layer(to_layer)

    loop(1, LAYERS, second_post)

    @pl.when(far == 0)
    def _():
        for to_layer in rest[3 :]:
            send_rows(to_layer)

    second_in[layer] = second_out[layer]
    second_got[layer] = second_stat[0]
    wait_all(second_out, second_in, LAYERS - 1, second_send, second_recv)
    wait_all(second_got, second_got, LAYERS - 1, second_stat_send, second_stat_recv)
    factors, _, total = join([second_got[i] for i in range(LAYERS)])
    hot = iota((8, HD), 1) == layer * 8 + iota((8, HD), 0)
    acc = None
    for i in range(LAYERS):
        term = second_in[i] * as_column(factors[i : i + 1], hot)
        acc = term if acc is None else acc + term
    normed = acc / as_column(total, hot)
    high = normed.astype(BF16)
    remain = normed - high.astype(F32)
    middle = remain.astype(BF16)
    low = (remain - middle.astype(F32)).astype(BF16)
    turned = (dot(low, signs) + dot(middle, signs) + dot(high, signs)) * root
    att_ref[0] = turned[0:STEPS].astype(BF16)
    att_ref[1] = turned[STEPS : 2 * STEPS].astype(BF16)

    far_copy.wait_send()
    keep.wait()
    wait_all(send, land_hbm, SEQ - 1, a2a_send, a2a_recv)


def finish_kernel(land_hbm, got_hbm, att_hbm, app_hbm, land, app, in_sems, out_sems, att_sem):
    att_copy = pltpu.make_async_copy(got_hbm, att_hbm, att_sem)
    att_copy.start()
    chunks = SEQ // 8
    for c in range(chunks):
        pltpu.make_async_copy(
            land_hbm.at[pl.ds(c * 8, 8)], land.at[pl.ds(c * 8, 8)], in_sems.at[c]
        ).start()
    to = iota((128, 128), 0)
    request, quarter = to // 64, lax.rem(to // 16, 4)
    source, rank = lax.rem(to // 2, 8), lax.rem(to, 2)
    wanted = source * 16 + request * 8 + quarter * 2 + rank
    move = jnp.where(iota((128, 128), 1) == wanted, 1.0, 0.0).astype(BF16)

    def out_copy(c):
        rows = pl.ds(c * 16, 16)
        return pltpu.make_async_copy(app.at[:, rows, :], app_hbm.at[:, rows, :], out_sems.at[c])

    for c in range(chunks):
        pltpu.make_async_copy(
            land_hbm.at[pl.ds(c * 8, 8)], land.at[pl.ds(c * 8, 8)], in_sems.at[c]
        ).wait()
        block = land[c * 8 : (c + 1) * 8].reshape(128, PIECE)
        moved = dot(move, block).astype(BF16)
        for r in range(REQ):
            for q in range(4):
                start = r * 64 + q * 16
                app[r, c * 16 : (c + 1) * 16, q * PIECE : (q + 1) * PIECE] = moved[start : start + 16]
        out_copy(c).start()
    for c in range(chunks):
        out_copy(c).wait()
    att_copy.wait()


def local(queries, cache_levels, scale_ids, scale_table, ctx_len, span_rows, span_len, owners):
    vmem, smem = pl.BlockSpec(memory_space=pltpu.VMEM), pl.BlockSpec(memory_space=pltpu.SMEM)
    anywhere = pl.BlockSpec(memory_space=pl.ANY)
    dma = pltpu.SemaphoreType.DMA
    turn = lambda x: jnp.swapaxes(x, -1, -2)
    landed, attended = pl.pallas_call(
        exchange_kernel,
        out_shape=(
            jax.ShapeDtypeStruct((SEQ, 16, PIECE), BF16),
            jax.ShapeDtypeStruct((REQ, STEPS, HD), BF16),
        ),
        in_specs=[anywhere, anywhere, smem, anywhere, smem, anywhere, smem, vmem],
        out_specs=(anywhere, vmem),
        scratch_shapes=[
            pltpu.VMEM((REQ, STEPS, HQ * HD), BF16),
            pltpu.VMEM((REQ, SLOT, WIDTH), BF16),
            pltpu.VMEM((REQ, SPAN, WIDTH), BF16),
            pltpu.VMEM((SEQ, 16, PIECE), BF16),
            pltpu.VMEM((2, BATCH_Y, NSCALE, 256), F32),
            pltpu.VMEM((2, BATCH_Y, REQ * (SLOT // GROUP), 256), F32),
            pltpu.VMEM((HQ * 8, HD), BF16),
            pltpu.VMEM((64, REQ * (SLOT + SPAN)), F32),
            pltpu.VMEM((PLANE, 64, HD), F32),
            pltpu.VMEM((PLANE, 64, HD), F32),
            pltpu.VMEM((PLANE, 2, HD), F32),
            pltpu.VMEM((PLANE, 2, HD), F32),
            pltpu.VMEM((LAYERS, 8, HD), F32),
            pltpu.VMEM((LAYERS, 8, HD), F32),
            pltpu.VMEM((1, 2, HD), F32),
            pltpu.VMEM((LAYERS, 2, HD), F32),
        ]
        + [dma] * 21
        + [pltpu.SemaphoreType.REGULAR((LAYERS,))],
        compiler_params=pltpu.CompilerParams(
            collective_id=0, has_side_effects=True, vmem_limit_bytes=VMEM
        ),
        cost_estimate=pl.CostEstimate(
            flops=2 * 10**9, bytes_accessed=5 * 2**20, transcendentals=400000
        ),
        name="exchange",
    )(
        queries, cache_levels, scale_ids, scale_table,
        turn(ctx_len), span_rows, turn(span_len), turn(owners),
    )
    return pl.pallas_call(
        finish_kernel,
        out_shape=(
            jax.ShapeDtypeStruct((REQ, STEPS, HD), BF16),
            jax.ShapeDtypeStruct((REQ, SEQ * CAP, WIDTH), BF16),
        ),
        in_specs=[anywhere, anywhere],
        out_specs=(anywhere, anywhere),
        scratch_shapes=[
            pltpu.VMEM((SEQ, 16, PIECE), BF16),
            pltpu.VMEM((REQ, SEQ * CAP, WIDTH), BF16),
            dma((8,)),
            dma((8,)),
            dma,
        ],
        compiler_params=pltpu.CompilerParams(vmem_limit_bytes=VMEM),
        name="finish",
    )(landed, attended)


def solution(mesh):
    return jax.shard_map(
        local,
        mesh=mesh,
        in_specs=(
            P("batch", None, None),
            P("batch", "seq", None),
            P("batch", "seq"),
            P(None, "batch"),
            P("batch", "seq"),
            P("batch", "seq", None),
            P("batch", "seq"),
            P("batch", "seq", None),
        ),
        out_specs=(P("batch", None, "seq"), P("batch", "seq", None)),
        check_vma=False,
    )
```

```python
import functools

import jax
import jax.numpy as jnp
from jax import lax
from jax.experimental import pallas as pl
from jax.experimental.pallas import tpu as pltpu
from jax.sharding import PartitionSpec as P

HQ = 64
KVH = 8
HD = 128
G = 8
CAP = 2
GROUP = 32
NSCALE = 16
STEPS = 4
SLOT = 256
SPAN = 64
REQ = 2
WIDTH = 2 * KVH * HD
SEQ = 64
PLANE = 8
LAYERS = 8
BATCH_Y = 4
PIECE = WIDTH // 4
VMEM = 60 * 2**20
MESH = pl.DeviceIdType.MESH
F32 = jnp.float32
BF16 = jnp.bfloat16


def iota(shape, axis):
    return lax.broadcasted_iota(jnp.int32, shape, axis)


def hadamard_signs():
    common = jnp.bitwise_and(iota((HD, HD), 0), iota((HD, HD), 1))
    parity = jnp.zeros((HD, HD), jnp.int32)
    for bit in range(7):
        parity = parity + jnp.bitwise_and(jnp.right_shift(common, bit), 1)
    return (1 - 2 * jnp.bitwise_and(parity, 1)).astype(F32).astype(BF16)


def dot(a, b, contract=((1,), (0,))):
    return lax.dot_general(a, b, (contract, ((), ())), preferred_element_type=F32)


def as_column(row, hot):
    return jnp.sum(jnp.where(hot, jnp.broadcast_to(row, hot.shape), 0.0), axis=1, keepdims=True)


def join(stats):
    tops = jnp.concatenate([stat[0:1] for stat in stats], axis=0)
    totals = jnp.concatenate([stat[1:2] for stat in stats], axis=0)
    top = jnp.max(tops, axis=0, keepdims=True)
    factors = jnp.exp(tops - top)
    return factors, top, jnp.sum(totals * factors, axis=0, keepdims=True)


def exchange_kernel(
    q_hbm, lev_hbm, ids_hbm, tab_hbm, ctx_hbm, span_hbm, slen_hbm, own_hbm,
    land_hbm, att_hbm,
    ids_ref, ctx_ref, slen_ref, own_ref, att_ref,
    q_ref, lev, span, send, tbl, scales, qrot, mask,
    first_out, first_in, first_stat, first_got, second_out, second_in, second_stat, second_got,
    small_sems, q_sem, tab_sem, lev_sem, span_sem, own_sem,
    a2a_send, a2a_recv, far_send, far_recv, near_send, near_recv, side_send, side_recv,
    first_send, first_recv, first_stat_send, first_stat_recv,
    second_send, second_recv, second_stat_send, second_stat_recv,
    ready, joined,
):
    me = lax.axis_index("seq")
    layer, place = me // PLANE, lax.rem(me, PLANE)
    batch = lax.axis_index("batch")
    far, row = batch // BATCH_Y, lax.rem(batch, BATCH_Y)
    partner = lax.rem(batch + BATCH_Y, 2 * BATCH_Y)
    sides = [far * BATCH_Y + lax.rem(row + i, BATCH_Y) for i in range(1, BATCH_Y)]
    lower = layer < LAYERS // 2

    def loop(start, stop, body):
        def step(i, carry):
            body(i)
            return carry

        lax.fori_loop(start, stop, step, 0)

    barrier = pltpu.get_barrier_semaphore()

    def greet(to):
        pl.semaphore_signal(barrier, inc=1, device_id=to, device_id_type=MESH)

    loop(1, PLANE, lambda i: greet({"seq": layer * PLANE + lax.rem(place + i, PLANE)}))
    for side in sides:
        greet({"batch": side})

    at_end = (layer == 0) | (layer == LAYERS - 1)
    sender = {"seq": jnp.where(lower, LAYERS - 1, 0) * PLANE + place, "batch": partner}

    def taker(i):
        return {
            "seq": (jnp.where(layer == 0, LAYERS // 2, 0) + i) * PLANE + place,
            "batch": partner,
        }

    @pl.when(far == 0)
    def _():
        greet(sender)
        pl.when(at_end)(lambda: loop(0, LAYERS // 2, lambda i: greet(taker(i))))

    loop((layer + 1) * PLANE, SEQ, lambda i: greet({"seq": i}))

    small = [
        pltpu.make_async_copy(here, there, small_sems.at[i])
        for i, (here, there) in enumerate(
            ((own_hbm, own_ref), (slen_hbm, slen_ref), (ctx_hbm, ctx_ref), (ids_hbm, ids_ref))
        )
    ]
    for copy in small:
        copy.start()
    span_copy = pltpu.make_async_copy(span_hbm, span, span_sem)
    span_copy.start()
    tab_copy = pltpu.make_async_copy(tab_hbm, tbl.at[far, row], tab_sem)
    tab_copy.start()
    q_copy = pltpu.make_async_copy(q_hbm, q_ref, q_sem)
    q_copy.start()
    lev_copy = pltpu.make_async_copy(lev_hbm, lev, lev_sem)
    lev_copy.start()

    for copy in small:
        copy.wait()
    owner_row = jnp.concatenate([own_ref[0], own_ref[1]], axis=1).astype(F32)
    above, along = iota((2 * SPAN, 2 * SPAN), 0), iota((2 * SPAN, 2 * SPAN), 1)
    owner_wide = jnp.broadcast_to(owner_row, (2 * SPAN, 2 * SPAN))
    owner_col = jnp.sum(jnp.where(above == along, owner_wide, 0.0), axis=1, keepdims=True)
    same = (owner_wide == owner_col) & (above < along) & (above // SPAN == along // SPAN)
    rank = jnp.sum(jnp.where(same, 1.0, 0.0), axis=0, keepdims=True)
    lane = iota((1, 2 * SPAN), 1)
    request = lane // SPAN
    kept = lax.rem(lane, SPAN) < jnp.where(request == 0, slen_ref[0, 0], slen_ref[0, 1])
    target = owner_row.astype(jnp.int32) * 16 + request * 8 + rank.astype(jnp.int32)
    target = jnp.concatenate(
        [jnp.where(kept, target + 2 * quarter, -1) for quarter in range(4)], axis=1
    )
    span_copy.wait()
    stacked = jnp.concatenate(
        [
            span[r, :, quarter * PIECE : (quarter + 1) * PIECE]
            for quarter in range(4)
            for r in range(REQ)
        ],
        axis=0,
    )
    for to_layer in range(LAYERS):
        rows = iota((16 * PLANE, REQ * SPAN * 4), 0) + to_layer * (16 * PLANE)
        pick = jnp.where(rows == target, 1.0, 0.0).astype(BF16)
        block = dot(pick, stacked).astype(BF16)
        send[pl.ds(to_layer * PLANE, PLANE)] = block.reshape(PLANE, 16, PIECE)

    known = far * (1 + jnp.where(at_end, LAYERS // 2, 0))
    pl.semaphore_wait(barrier, PLANE - 1 + BATCH_Y - 1 + layer * PLANE + known)

    loop(
        0,
        layer,
        lambda i: pl.semaphore_signal(
            ready.at[layer], inc=1, device_id={"seq": i * PLANE + place}, device_id_type=MESH
        ),
    )

    tab_copy.wait()
    def to_other_half():
        def one(i):
            pltpu.make_async_remote_copy(
                src_ref=tbl.at[far, row], dst_ref=tbl.at[far, row],
                send_sem=far_send, recv_sem=far_recv, device_id=taker(i), device_id_type=MESH,
            ).start()

        loop(0, LAYERS // 2, one)

    @pl.when(far == 1)
    def _():
        pl.when(at_end)(to_other_half)
        pl.semaphore_signal(joined, inc=1, device_id=sender, device_id_type=MESH)

    def to_sides(half, send_sem, recv_sem):
        for side in sides:
            pltpu.make_async_remote_copy(
                src_ref=tbl.at[half, row], dst_ref=tbl.at[half, row],
                send_sem=send_sem, recv_sem=recv_sem,
                device_id={"batch": side}, device_id_type=MESH,
            ).start()

    def from_sides(send_sem, recv_sem):
        some = tbl.at[0, pl.ds(0, BATCH_Y - 1)]
        every = pltpu.make_async_remote_copy(
            src_ref=some, dst_ref=some, send_sem=send_sem, recv_sem=recv_sem,
            device_id={"batch": partner}, device_id_type=MESH,
        )
        every.wait_send()
        every.wait_recv()

    to_sides(far, near_send, near_recv)

    def await_layer(to_layer):
        pl.when(to_layer > layer)(lambda: pl.semaphore_wait(ready.at[to_layer], 1))

    def send_rows(to_layer, start=0):
        def one(i):
            to = to_layer * PLANE + lax.rem(place + i, PLANE)
            pltpu.make_async_remote_copy(
                src_ref=send.at[to], dst_ref=land_hbm.at[me], send_sem=a2a_send, recv_sem=a2a_recv,
                device_id={"seq": to}, device_id_type=MESH,
            ).start()

        loop(start, PLANE, one)

    def post(to_layer):
        await_layer(to_layer)
        send_rows(to_layer)

    half = LAYERS // 2
    own = jnp.where(lower, layer, LAYERS - 1 - layer)

    def counted(number):
        return jnp.where(lower, number, LAYERS - 1 - number)

    across = [counted(half + i) for i in (0, 3, 1, 2)]

    def post_inner():
        for number in range(half - 1, 0, -1):
            pl.when(number > own)(functools.partial(post, counted(number)))

    def post_outer():
        for number in range(half - 2, -1, -1):
            pl.when(number < own)(functools.partial(post, counted(number)))

    def post_some(layers):
        for to_layer in layers:
            post(to_layer)

    post_inner()
    post_some(across)
    send_rows(layer, 1)
    post_outer()
    keep = pltpu.make_async_copy(send.at[me], land_hbm.at[me], own_sem)
    keep.start()

    @pl.when((far == 0) & at_end)
    def _():
        pl.semaphore_wait(joined, LAYERS // 2)
        to_other_half()

    signs = hadamard_signs()
    root = jnp.float32(1.0) / jnp.sqrt(jnp.float32(HD))
    q_copy.wait()
    queries = jnp.concatenate([q_ref[0].astype(F32), q_ref[1].astype(F32)], axis=0)
    stacked_q = jnp.concatenate(
        [queries[:, h * HD : (h + 1) * HD] for h in range(HQ)], axis=0
    ).astype(BF16)
    qrot[...] = (dot(stacked_q, signs) * root).astype(BF16)

    keys = REQ * (SLOT + SPAN)
    wanted = lax.rem(iota((64, keys), 0) // STEPS, REQ)
    column = iota((64, keys), 1)
    in_slot = column < REQ * SLOT
    other = column - REQ * SLOT
    key_request = jnp.where(in_slot, column // SLOT, other // SPAN)
    position = jnp.where(in_slot, lax.rem(column, SLOT), lax.rem(other, SPAN))
    first = key_request == 0
    limit = jnp.where(
        in_slot,
        jnp.where(first, ctx_ref[0, 0], ctx_ref[0, 1]),
        jnp.where(first, slen_ref[0, 0], slen_ref[0, 1]),
    )
    mask[...] = jnp.where((wanted == key_request) & (position < limit), 1.0, 0.0)
    blocks = REQ * (SLOT // GROUP)
    group = jnp.zeros((blocks, 3 * NSCALE), jnp.int32)
    for r in range(REQ):
        for b in range(SLOT // GROUP):
            here = iota((blocks, 3 * NSCALE), 0) == r * (SLOT // GROUP) + b
            group = jnp.where(here, ids_ref[r, b], group)
    chosen = jnp.where(lax.rem(iota((blocks, 3 * NSCALE), 1), NSCALE) == group, 1.0, 0.0).astype(BF16)

    pltpu.make_async_remote_copy(
        src_ref=tbl.at[0, 0], dst_ref=tbl.at[0, 0], send_sem=far_send, recv_sem=far_recv,
        device_id={"batch": partner}, device_id_type=MESH,
    ).wait_recv()
    to_sides(1 - far, side_send, side_recv)
    from_sides(near_send, near_recv)
    from_sides(side_send, side_recv)

    for f in range(2):
        for r in range(BATCH_Y):
            piece = tbl[f, r]
            high = piece.astype(BF16)
            remain = piece - high.astype(F32)
            middle = remain.astype(BF16)
            low = (remain - middle.astype(F32)).astype(BF16)
            scales[f, r] = dot(chosen, jnp.concatenate([high, middle, low], axis=0))
    lev_copy.wait()

    lane = iota((64, HD), 1)
    sub = lax.rem(iota((64, HD), 0), 8)

    def dequant(pair, half, base, part):
        pieces = []
        lanes = pl.ds(pl.multiple_of(base, HD), HD)
        for r in range(REQ):
            for b in range(SLOT // GROUP):
                at = r * (SLOT // GROUP) + b
                scale = scales[part, pair, at : at + 1, half * HD : (half + 1) * HD]
                level = lev[r, b * GROUP : (b + 1) * GROUP, lanes].astype(F32)
                pieces.append((level * scale).astype(BF16))
        for r in range(REQ):
            pieces.append(span[r, :, lanes])
        return jnp.concatenate(pieces, axis=0)

    def head_pair(pair, carry):
        tops, totals = carry
        for half in range(2):
            head = pair * 2 + half
            key_rows = dequant(pair, half, head * HD, 0)
            q = qrot[pl.ds(pl.multiple_of(head * 64, 64), 64), :]
            scores = dot(q, key_rows, ((1,), (1,))) * root
            scores = jnp.where(mask[...] > 0.0, scores, jnp.float32(-1e30))
            top = jnp.max(scores, axis=1, keepdims=True)
            weights = jnp.exp(scores - top)
            total = jnp.sum(weights, axis=1, keepdims=True)
            value_rows = dequant(pair, half, (KVH + head) * HD, 1)
            acc = dot(weights.astype(BF16), value_rows)
            hot = lane == head * 8 + sub
            tops = tops + jnp.sum(jnp.where(hot, top, 0.0).reshape(G, 8, HD), axis=1)
            totals = totals + jnp.sum(jnp.where(hot, total, 0.0).reshape(G, 8, HD), axis=1)
            at = pl.ds(pl.multiple_of(head * 8, 8), 8)
            for g in range(G):
                first_out[g, at, :] = acc[g * 8 : (g + 1) * 8]
        return tops, totals

    zeros = jnp.zeros((G, HD), F32)
    tops, totals = lax.fori_loop(0, KVH // 2, head_pair, (zeros, zeros))
    for g in range(G):
        first_stat[g, 0:1] = tops[g : g + 1]
        first_stat[g, 1:2] = totals[g : g + 1]

    def first_post(i):
        to = lax.rem(place + i, PLANE)
        for out, into, send_sem, recv_sem in (
            (first_out, first_in, first_send, first_recv),
            (first_stat, first_got, first_stat_send, first_stat_recv),
        ):
            pltpu.make_async_remote_copy(
                src_ref=out.at[to], dst_ref=into.at[place], send_sem=send_sem, recv_sem=recv_sem,
                device_id={"seq": layer * PLANE + to}, device_id_type=MESH,
            ).start()

    def wait_all(out, into, count, send_sem, recv_sem):
        every = pltpu.make_async_remote_copy(
            src_ref=out.at[pl.ds(0, count)], dst_ref=into.at[pl.ds(0, count)],
            send_sem=send_sem, recv_sem=recv_sem, device_id={"seq": me}, device_id_type=MESH,
        )
        every.wait_send()
        every.wait_recv()

    loop(1, PLANE, first_post)
    first_in[place] = first_out[place]
    first_got[place] = first_stat[place]
    wait_all(first_out, first_in, PLANE - 1, first_send, first_recv)
    wait_all(first_stat, first_got, PLANE - 1, first_stat_send, first_stat_recv)
    factors, top, total = join([first_got[i] for i in range(PLANE)])
    hot = lane == iota((64, HD), 0)
    acc = None
    for i in range(PLANE):
        term = first_in[i] * as_column(factors[i : i + 1], hot)
        acc = term if acc is None else acc + term
    second_out[...] = acc.reshape(LAYERS, 8, HD)
    second_stat[0, 0:1] = top
    second_stat[0, 1:2] = total

    def second_post(i):
        to = lax.rem(layer + i, LAYERS)
        for out, into, send_sem, recv_sem in (
            (second_out.at[to], second_in, second_send, second_recv),
            (second_stat.at[0], second_got, second_stat_send, second_stat_recv),
        ):
            pltpu.make_async_remote_copy(
                src_ref=out, dst_ref=into.at[layer], send_sem=send_sem, recv_sem=recv_sem,
                device_id={"seq": to * PLANE + place}, device_id_type=MESH,
            ).start()

    loop(1, LAYERS, second_post)
    second_in[layer] = second_out[layer]
    second_got[layer] = second_stat[0]
    wait_all(second_out, second_in, LAYERS - 1, second_send, second_recv)
    wait_all(second_got, second_got, LAYERS - 1, second_stat_send, second_stat_recv)
    factors, _, total = join([second_got[i] for i in range(LAYERS)])
    hot = iota((8, HD), 1) == layer * 8 + iota((8, HD), 0)
    acc = None
    for i in range(LAYERS):
        term = second_in[i] * as_column(factors[i : i + 1], hot)
        acc = term if acc is None else acc + term
    normed = acc / as_column(total, hot)
    high = normed.astype(BF16)
    remain = normed - high.astype(F32)
    middle = remain.astype(BF16)
    low = (remain - middle.astype(F32)).astype(BF16)
    turned = (dot(low, signs) + dot(middle, signs) + dot(high, signs)) * root
    att_ref[0] = turned[0:STEPS].astype(BF16)
    att_ref[1] = turned[STEPS : 2 * STEPS].astype(BF16)
    att_copy = pltpu.make_async_copy(att_ref, att_hbm, small_sems.at[0])
    att_copy.start()

    sent = pltpu.make_async_remote_copy(
        src_ref=tbl.at[0], dst_ref=tbl.at[0], send_sem=far_send, recv_sem=far_recv,
        device_id={"batch": partner}, device_id_type=MESH,
    )
    pl.when(at_end)(sent.wait_send)
    att_copy.wait()
    keep.wait()
    wait_all(send, land_hbm, SEQ - 1, a2a_send, a2a_recv)


def finish_kernel(land_hbm, got_hbm, att_hbm, app_hbm, land, app, in_sems, out_sems, att_sem):
    att_copy = pltpu.make_async_copy(got_hbm, att_hbm, att_sem)
    att_copy.start()
    chunks = SEQ // 8
    for c in range(chunks):
        pltpu.make_async_copy(
            land_hbm.at[pl.ds(c * 8, 8)], land.at[pl.ds(c * 8, 8)], in_sems.at[c]
        ).start()
    to = iota((128, 128), 0)
    request, quarter = to // 64, lax.rem(to // 16, 4)
    source, rank = lax.rem(to // 2, 8), lax.rem(to, 2)
    wanted = source * 16 + request * 8 + quarter * 2 + rank
    move = jnp.where(iota((128, 128), 1) == wanted, 1.0, 0.0).astype(BF16)

    def out_copy(c):
        rows = pl.ds(c * 16, 16)
        return pltpu.make_async_copy(app.at[:, rows, :], app_hbm.at[:, rows, :], out_sems.at[c])

    for c in range(chunks):
        pltpu.make_async_copy(
            land_hbm.at[pl.ds(c * 8, 8)], land.at[pl.ds(c * 8, 8)], in_sems.at[c]
        ).wait()
        block = land[c * 8 : (c + 1) * 8].reshape(128, PIECE)
        moved = dot(move, block).astype(BF16)
        for r in range(REQ):
            for q in range(4):
                start = r * 64 + q * 16
                app[r, c * 16 : (c + 1) * 16, q * PIECE : (q + 1) * PIECE] = moved[start : start + 16]
        out_copy(c).start()
    for c in range(chunks):
        out_copy(c).wait()
    att_copy.wait()


def local(queries, cache_levels, scale_ids, scale_table, ctx_len, span_rows, span_len, owners):
    anywhere = pl.BlockSpec(memory_space=pl.ANY)
    dma = pltpu.SemaphoreType.DMA
    turn = lambda x: jnp.swapaxes(x, -1, -2)
    landed, attended = pl.pallas_call(
        exchange_kernel,
        out_shape=(
            jax.ShapeDtypeStruct((SEQ, 16, PIECE), BF16),
            jax.ShapeDtypeStruct((REQ, STEPS, HD), BF16),
        ),
        in_specs=[anywhere] * 8,
        out_specs=(anywhere, anywhere),
        scratch_shapes=[
            pltpu.SMEM((REQ, SLOT // GROUP), jnp.int32),
            pltpu.SMEM((1, REQ), jnp.int32),
            pltpu.SMEM((1, REQ), jnp.int32),
            pltpu.VMEM((REQ, 1, SPAN), jnp.int32),
            pltpu.VMEM((REQ, STEPS, HD), BF16),
            pltpu.VMEM((REQ, STEPS, HQ * HD), BF16),
            pltpu.VMEM((REQ, SLOT, WIDTH), BF16),
            pltpu.VMEM((REQ, SPAN, WIDTH), BF16),
            pltpu.VMEM((SEQ, 16, PIECE), BF16),
            pltpu.VMEM((2, BATCH_Y, NSCALE, 256), F32),
            pltpu.VMEM((2, BATCH_Y, REQ * (SLOT // GROUP), 256), F32),
            pltpu.VMEM((HQ * 8, HD), BF16),
            pltpu.VMEM((64, REQ * (SLOT + SPAN)), F32),
            pltpu.VMEM((PLANE, 64, HD), F32),
            pltpu.VMEM((PLANE, 64, HD), F32),
            pltpu.VMEM((PLANE, 2, HD), F32),
            pltpu.VMEM((PLANE, 2, HD), F32),
            pltpu.VMEM((LAYERS, 8, HD), F32),
            pltpu.VMEM((LAYERS, 8, HD), F32),
            pltpu.VMEM((1, 2, HD), F32),
            pltpu.VMEM((LAYERS, 2, HD), F32),
        ]
        + [dma((4,))]
        + [dma] * 21
        + [pltpu.SemaphoreType.REGULAR((LAYERS,)), pltpu.SemaphoreType.REGULAR],
        compiler_params=pltpu.CompilerParams(
            collective_id=0, has_side_effects=True, vmem_limit_bytes=VMEM
        ),
        cost_estimate=pl.CostEstimate(
            flops=2 * 10**9, bytes_accessed=5 * 2**20, transcendentals=400000
        ),
        name="exchange",
    )(
        queries, cache_levels, scale_ids, scale_table,
        turn(ctx_len), span_rows, turn(span_len), turn(owners),
    )
    return pl.pallas_call(
        finish_kernel,
        out_shape=(
            jax.ShapeDtypeStruct((REQ, STEPS, HD), BF16),
            jax.ShapeDtypeStruct((REQ, SEQ * CAP, WIDTH), BF16),
        ),
        in_specs=[anywhere, anywhere],
        out_specs=(anywhere, anywhere),
        scratch_shapes=[
            pltpu.VMEM((SEQ, 16, PIECE), BF16),
            pltpu.VMEM((REQ, SEQ * CAP, WIDTH), BF16),
            dma((8,)),
            dma((8,)),
            dma,
        ],
        compiler_params=pltpu.CompilerParams(vmem_limit_bytes=VMEM),
        name="finish",
    )(landed, attended)


def solution(mesh):
    return jax.shard_map(
        local,
        mesh=mesh,
        in_specs=(
            P("batch", None, None),
            P("batch", "seq", None),
            P("batch", "seq"),
            P(None, "batch"),
            P("batch", "seq"),
            P("batch", "seq", None),
            P("batch", "seq"),
            P("batch", "seq", None),
        ),
        out_specs=(P("batch", None, "seq"), P("batch", "seq", None)),
        check_vma=False,
    )
```

```python
import functools

import jax
import jax.numpy as jnp
from jax import lax
from jax.experimental import pallas as pl
from jax.experimental.pallas import tpu as pltpu
from jax.sharding import PartitionSpec as P

HQ = 64
KVH = 8
HD = 128
G = 8
CAP = 2
GROUP = 32
NSCALE = 16
STEPS = 4
SLOT = 256
SPAN = 64
REQ = 2
WIDTH = 2 * KVH * HD
SEQ = 64
PLANE = 8
LAYERS = 8
BATCH_Y = 4
PIECE = WIDTH // 4
VMEM = 60 * 2**20
MESH = pl.DeviceIdType.MESH
F32 = jnp.float32
BF16 = jnp.bfloat16


def iota(shape, axis):
    return lax.broadcasted_iota(jnp.int32, shape, axis)


def hadamard_signs():
    common = jnp.bitwise_and(iota((HD, HD), 0), iota((HD, HD), 1))
    parity = jnp.zeros((HD, HD), jnp.int32)
    for bit in range(7):
        parity = parity + jnp.bitwise_and(jnp.right_shift(common, bit), 1)
    return (1 - 2 * jnp.bitwise_and(parity, 1)).astype(F32).astype(BF16)


def dot(a, b, contract=((1,), (0,))):
    return lax.dot_general(a, b, (contract, ((), ())), preferred_element_type=F32)


def as_column(row, hot):
    return jnp.sum(jnp.where(hot, jnp.broadcast_to(row, hot.shape), 0.0), axis=1, keepdims=True)


def join(stats):
    tops = jnp.concatenate([stat[0:1] for stat in stats], axis=0)
    totals = jnp.concatenate([stat[1:2] for stat in stats], axis=0)
    top = jnp.max(tops, axis=0, keepdims=True)
    factors = jnp.exp(tops - top)
    return factors, top, jnp.sum(totals * factors, axis=0, keepdims=True)


def exchange_kernel(
    q_hbm, lev_hbm, ids_hbm, tab_hbm, ctx_hbm, span_hbm, slen_hbm, own_hbm,
    app_hbm, att_hbm,
    land, app, ids_ref, ctx_ref, slen_ref, own_ref, att_ref,
    q_ref, lev, span, send, tbl, scales, qrot, mask,
    first_out, first_in, first_stat, first_got, second_out, second_in, second_stat, second_got,
    small_sems, q_sem, tab_sem, lev_sem, span_sem, app_sems,
    a2a_send, a2a_recv, far_send, far_recv, near_send, near_recv, side_send, side_recv,
    first_send, first_recv, first_stat_send, first_stat_recv,
    second_send, second_recv, second_stat_send, second_stat_recv,
    ready, joined,
):
    me = lax.axis_index("seq")
    layer, place = me // PLANE, lax.rem(me, PLANE)
    batch = lax.axis_index("batch")
    far, row = batch // BATCH_Y, lax.rem(batch, BATCH_Y)
    partner = lax.rem(batch + BATCH_Y, 2 * BATCH_Y)
    sides = [far * BATCH_Y + lax.rem(row + i, BATCH_Y) for i in range(1, BATCH_Y)]
    lower = layer < LAYERS // 2

    def loop(start, stop, body):
        def step(i, carry):
            body(i)
            return carry

        lax.fori_loop(start, stop, step, 0)

    barrier = pltpu.get_barrier_semaphore()

    def greet(to):
        pl.semaphore_signal(barrier, inc=1, device_id=to, device_id_type=MESH)

    loop(1, PLANE, lambda i: greet({"seq": layer * PLANE + lax.rem(place + i, PLANE)}))
    for side in sides:
        greet({"batch": side})

    at_end = (layer == 0) | (layer == LAYERS - 1)
    sender = {"seq": jnp.where(lower, LAYERS - 1, 0) * PLANE + place, "batch": partner}

    def taker(i):
        return {
            "seq": (jnp.where(layer == 0, LAYERS // 2, 0) + i) * PLANE + place,
            "batch": partner,
        }

    @pl.when(far == 0)
    def _():
        greet(sender)
        pl.when(at_end)(lambda: loop(0, LAYERS // 2, lambda i: greet(taker(i))))

    loop((layer + 1) * PLANE, SEQ, lambda i: greet({"seq": i}))
    pl.when(far == 1)(lambda: loop(0, layer * PLANE, lambda i: greet({"seq": i})))

    small = [
        pltpu.make_async_copy(here, there, small_sems.at[i])
        for i, (here, there) in enumerate(
            ((own_hbm, own_ref), (slen_hbm, slen_ref), (ctx_hbm, ctx_ref), (ids_hbm, ids_ref))
        )
    ]
    for copy in small:
        copy.start()
    span_copy = pltpu.make_async_copy(span_hbm, span, span_sem)
    span_copy.start()
    tab_copy = pltpu.make_async_copy(tab_hbm, tbl.at[far, row], tab_sem)
    tab_copy.start()
    q_copy = pltpu.make_async_copy(q_hbm, q_ref, q_sem)
    q_copy.start()
    lev_copy = pltpu.make_async_copy(lev_hbm, lev, lev_sem)
    lev_copy.start()

    for copy in small:
        copy.wait()
    owner_row = jnp.concatenate([own_ref[0], own_ref[1]], axis=1).astype(F32)
    above, along = iota((2 * SPAN, 2 * SPAN), 0), iota((2 * SPAN, 2 * SPAN), 1)
    owner_wide = jnp.broadcast_to(owner_row, (2 * SPAN, 2 * SPAN))
    owner_col = jnp.sum(jnp.where(above == along, owner_wide, 0.0), axis=1, keepdims=True)
    same = (owner_wide == owner_col) & (above < along) & (above // SPAN == along // SPAN)
    rank = jnp.sum(jnp.where(same, 1.0, 0.0), axis=0, keepdims=True)
    lane = iota((1, 2 * SPAN), 1)
    request = lane // SPAN
    kept = lax.rem(lane, SPAN) < jnp.where(request == 0, slen_ref[0, 0], slen_ref[0, 1])
    target = owner_row.astype(jnp.int32) * 16 + request * 8 + rank.astype(jnp.int32)
    target = jnp.concatenate(
        [jnp.where(kept, target + 2 * quarter, -1) for quarter in range(4)], axis=1
    )
    span_copy.wait()
    stacked = jnp.concatenate(
        [
            span[r, :, quarter * PIECE : (quarter + 1) * PIECE]
            for quarter in range(4)
            for r in range(REQ)
        ],
        axis=0,
    )
    for to_layer in range(LAYERS):
        rows = iota((16 * PLANE, REQ * SPAN * 4), 0) + to_layer * (16 * PLANE)
        pick = jnp.where(rows == target, 1.0, 0.0).astype(BF16)
        block = dot(pick, stacked).astype(BF16)
        send[pl.ds(to_layer * PLANE, PLANE)] = block.reshape(PLANE, 16, PIECE)

    known = far * (1 + jnp.where(at_end, LAYERS // 2, 0))
    layers_known = jnp.where(far == 0, layer, LAYERS - 1)
    pl.semaphore_wait(barrier, PLANE - 1 + BATCH_Y - 1 + layers_known * PLANE + known)

    loop(
        0,
        jnp.where(far == 0, layer, 0),
        lambda i: pl.semaphore_signal(
            ready.at[layer], inc=1, device_id={"seq": i * PLANE + place}, device_id_type=MESH
        ),
    )

    tab_copy.wait()
    def to_other_half():
        def one(i):
            pltpu.make_async_remote_copy(
                src_ref=tbl.at[far, row], dst_ref=tbl.at[far, row],
                send_sem=far_send, recv_sem=far_recv, device_id=taker(i), device_id_type=MESH,
            ).start()

        loop(0, LAYERS // 2, one)

    @pl.when(far == 1)
    def _():
        pl.when(at_end)(to_other_half)
        pl.semaphore_signal(joined, inc=1, device_id=sender, device_id_type=MESH)

    def to_sides(half, send_sem, recv_sem):
        for side in sides:
            pltpu.make_async_remote_copy(
                src_ref=tbl.at[half, row], dst_ref=tbl.at[half, row],
                send_sem=send_sem, recv_sem=recv_sem,
                device_id={"batch": side}, device_id_type=MESH,
            ).start()

    def from_sides(send_sem, recv_sem):
        some = tbl.at[0, pl.ds(0, BATCH_Y - 1)]
        every = pltpu.make_async_remote_copy(
            src_ref=some, dst_ref=some, send_sem=send_sem, recv_sem=recv_sem,
            device_id={"batch": partner}, device_id_type=MESH,
        )
        every.wait_send()
        every.wait_recv()

    to_sides(far, near_send, near_recv)

    def await_layer(to_layer):
        pl.when((to_layer > layer) & (far == 0))(lambda: pl.semaphore_wait(ready.at[to_layer], 1))

    def send_rows(to_layer, start=0):
        def one(i):
            to = to_layer * PLANE + lax.rem(place + i, PLANE)
            pltpu.make_async_remote_copy(
                src_ref=send.at[to], dst_ref=land.at[me], send_sem=a2a_send, recv_sem=a2a_recv.at[layer],
                device_id={"seq": to}, device_id_type=MESH,
            ).start()

        loop(start, PLANE, one)

    def post(to_layer):
        await_layer(to_layer)
        send_rows(to_layer)

    half = LAYERS // 2
    own = jnp.where(lower, layer, LAYERS - 1 - layer)

    def counted(number):
        return jnp.where(lower, number, LAYERS - 1 - number)

    across = [
        jnp.where(lower, half + up, half - 1 - jnp.where(far == 0, down, other))
        for up, down, other in zip((0, 3, 2, 1), (3, 2, 1, 0), (0, 3, 2, 1))
    ]

    def post_inner():
        for number in range(half - 1, 0, -1):
            pl.when(number > own)(functools.partial(post, counted(number)))

    def each_outer(act):
        for number in range(half - 2, -1, -1):
            pl.when(number < own)(functools.partial(act, counted(number)))

    def post_some(layers):
        for to_layer in layers:
            post(to_layer)

    post_inner()
    post_some(across[: 3])
    send_rows(layer, 1)
    each_outer(post)
    land[me] = send[me]

    @pl.when((far == 0) & at_end)
    def _():
        pl.semaphore_wait(joined, LAYERS // 2)
        to_other_half()

    signs = hadamard_signs()
    root = jnp.float32(1.0) / jnp.sqrt(jnp.float32(HD))
    q_copy.wait()
    queries = jnp.concatenate([q_ref[0].astype(F32), q_ref[1].astype(F32)], axis=0)
    stacked_q = jnp.concatenate(
        [queries[:, h * HD : (h + 1) * HD] for h in range(HQ)], axis=0
    ).astype(BF16)
    qrot[...] = (dot(stacked_q, signs) * root).astype(BF16)

    keys = REQ * (SLOT + SPAN)
    wanted = lax.rem(iota((64, keys), 0) // STEPS, REQ)
    column = iota((64, keys), 1)
    in_slot = column < REQ * SLOT
    other = column - REQ * SLOT
    key_request = jnp.where(in_slot, column // SLOT, other // SPAN)
    position = jnp.where(in_slot, lax.rem(column, SLOT), lax.rem(other, SPAN))
    first = key_request == 0
    limit = jnp.where(
        in_slot,
        jnp.where(first, ctx_ref[0, 0], ctx_ref[0, 1]),
        jnp.where(first, slen_ref[0, 0], slen_ref[0, 1]),
    )
    mask[...] = jnp.where((wanted == key_request) & (position < limit), 1.0, 0.0)
    blocks = REQ * (SLOT // GROUP)
    group = jnp.zeros((blocks, 3 * NSCALE), jnp.int32)
    for r in range(REQ):
        for b in range(SLOT // GROUP):
            here = iota((blocks, 3 * NSCALE), 0) == r * (SLOT // GROUP) + b
            group = jnp.where(here, ids_ref[r, b], group)
    chosen = jnp.where(lax.rem(iota((blocks, 3 * NSCALE), 1), NSCALE) == group, 1.0, 0.0).astype(BF16)

    pltpu.make_async_remote_copy(
        src_ref=tbl.at[0, 0], dst_ref=tbl.at[0, 0], send_sem=far_send, recv_sem=far_recv,
        device_id={"batch": partner}, device_id_type=MESH,
    ).wait_recv()
    to_sides(1 - far, side_send, side_recv)
    from_sides(near_send, near_recv)
    from_sides(side_send, side_recv)

    for f in range(2):
        for r in range(BATCH_Y):
            piece = tbl[f, r]
            high = piece.astype(BF16)
            remain = piece - high.astype(F32)
            middle = remain.astype(BF16)
            low = (remain - middle.astype(F32)).astype(BF16)
            scales[f, r] = dot(chosen, jnp.concatenate([high, middle, low], axis=0))
    lev_copy.wait()

    lane = iota((64, HD), 1)
    sub = lax.rem(iota((64, HD), 0), 8)

    def dequant(pair, half, base, part):
        pieces = []
        lanes = pl.ds(pl.multiple_of(base, HD), HD)
        for r in range(REQ):
            for b in range(SLOT // GROUP):
                at = r * (SLOT // GROUP) + b
                scale = scales[part, pair, at : at + 1, half * HD : (half + 1) * HD]
                level = lev[r, b * GROUP : (b + 1) * GROUP, lanes].astype(F32)
                pieces.append((level * scale).astype(BF16))
        for r in range(REQ):
            pieces.append(span[r, :, lanes])
        return jnp.concatenate(pieces, axis=0)

    def head_pair(pair, carry):
        tops, totals = carry
        for half in range(2):
            head = pair * 2 + half
            key_rows = dequant(pair, half, head * HD, 0)
            q = qrot[pl.ds(pl.multiple_of(head * 64, 64), 64), :]
            scores = dot(q, key_rows, ((1,), (1,))) * root
            scores = jnp.where(mask[...] > 0.0, scores, jnp.float32(-1e30))
            top = jnp.max(scores, axis=1, keepdims=True)
            weights = jnp.exp(scores - top)
            total = jnp.sum(weights, axis=1, keepdims=True)
            value_rows = dequant(pair, half, (KVH + head) * HD, 1)
            acc = dot(weights.astype(BF16), value_rows)
            hot = lane == head * 8 + sub
            tops = tops + jnp.sum(jnp.where(hot, top, 0.0).reshape(G, 8, HD), axis=1)
            totals = totals + jnp.sum(jnp.where(hot, total, 0.0).reshape(G, 8, HD), axis=1)
            at = pl.ds(pl.multiple_of(head * 8, 8), 8)
            for g in range(G):
                first_out[g, at, :] = acc[g * 8 : (g + 1) * 8]
        return tops, totals

    zeros = jnp.zeros((G, HD), F32)
    tops, totals = lax.fori_loop(0, KVH // 2, head_pair, (zeros, zeros))
    for g in range(G):
        first_stat[g, 0:1] = tops[g : g + 1]
        first_stat[g, 1:2] = totals[g : g + 1]

    def first_post(i):
        to = lax.rem(place + i, PLANE)
        for out, into, send_sem, recv_sem in (
            (first_out, first_in, first_send, first_recv),
            (first_stat, first_got, first_stat_send, first_stat_recv),
        ):
            pltpu.make_async_remote_copy(
                src_ref=out.at[to], dst_ref=into.at[place], send_sem=send_sem, recv_sem=recv_sem,
                device_id={"seq": layer * PLANE + to}, device_id_type=MESH,
            ).start()

    def wait_all(out, into, count, send_sem, recv_sem):
        every = pltpu.make_async_remote_copy(
            src_ref=out.at[pl.ds(0, count)], dst_ref=into.at[pl.ds(0, count)],
            send_sem=send_sem, recv_sem=recv_sem, device_id={"seq": me}, device_id_type=MESH,
        )
        every.wait_send()
        every.wait_recv()

    loop(1, PLANE, first_post)
    first_in[place] = first_out[place]
    first_got[place] = first_stat[place]
    wait_all(first_out, first_in, PLANE - 1, first_send, first_recv)
    wait_all(first_stat, first_got, PLANE - 1, first_stat_send, first_stat_recv)
    factors, top, total = join([first_got[i] for i in range(PLANE)])
    hot = lane == iota((64, HD), 0)
    acc = None
    for i in range(PLANE):
        term = first_in[i] * as_column(factors[i : i + 1], hot)
        acc = term if acc is None else acc + term
    second_out[...] = acc.reshape(LAYERS, 8, HD)
    second_stat[0, 0:1] = top
    second_stat[0, 1:2] = total

    def second_post(i):
        to = lax.rem(layer + i, LAYERS)
        for out, into, send_sem, recv_sem in (
            (second_out.at[to], second_in, second_send, second_recv),
            (second_stat.at[0], second_got, second_stat_send, second_stat_recv),
        ):
            pltpu.make_async_remote_copy(
                src_ref=out, dst_ref=into.at[layer], send_sem=send_sem, recv_sem=recv_sem,
                device_id={"seq": to * PLANE + place}, device_id_type=MESH,
            ).start()

    for to_layer in across[3 :]:
        await_layer(to_layer)
    loop(1, LAYERS, second_post)
    for to_layer in across[3 :]:
        send_rows(to_layer)
    second_in[layer] = second_out[layer]
    second_got[layer] = second_stat[0]
    to = iota((128, 128), 0)
    request, quarter = to // 64, lax.rem(to // 16, 4)
    source, rank = lax.rem(to // 2, 8), lax.rem(to, 2)
    wanted = source * 16 + request * 8 + quarter * 2 + rank
    move = jnp.where(iota((128, 128), 1) == wanted, 1.0, 0.0).astype(BF16)

    def out_copy(at):
        rows = pl.ds(pl.multiple_of(at * 16, 16), 16)
        return pltpu.make_async_copy(app.at[:, rows, :], app_hbm.at[:, rows, :], app_sems.at[at])

    def place_layer(at, count):
        some = land.at[pl.ds(0, count)]
        pltpu.make_async_remote_copy(
            src_ref=some, dst_ref=some, send_sem=a2a_send, recv_sem=a2a_recv.at[at],
            device_id={"seq": me}, device_id_type=MESH,
        ).wait_recv()
        block = land[pl.ds(at * PLANE, PLANE)].reshape(128, PIECE)
        moved = dot(move, block).astype(BF16)
        rows = pl.ds(pl.multiple_of(at * 16, 16), 16)
        for r in range(REQ):
            for q in range(4):
                start = r * 64 + q * 16
                app[r, rows, q * PIECE : (q + 1) * PIECE] = moved[start : start + 16]
        out_copy(at).start()

    place_layer(layer, PLANE - 1)
    for i in range(1, half):
        place_layer(layer // half * half + lax.rem(layer + i, half), PLANE)
    for i in range(half):
        place_layer(counted(LAYERS - 1 - i), PLANE)
    wait_all(second_out, second_in, LAYERS - 1, second_send, second_recv)
    wait_all(second_got, second_got, LAYERS - 1, second_stat_send, second_stat_recv)
    factors, _, total = join([second_got[i] for i in range(LAYERS)])
    hot = iota((8, HD), 1) == layer * 8 + iota((8, HD), 0)
    acc = None
    for i in range(LAYERS):
        term = second_in[i] * as_column(factors[i : i + 1], hot)
        acc = term if acc is None else acc + term
    normed = acc / as_column(total, hot)
    high = normed.astype(BF16)
    remain = normed - high.astype(F32)
    middle = remain.astype(BF16)
    low = (remain - middle.astype(F32)).astype(BF16)
    turned = (dot(low, signs) + dot(middle, signs) + dot(high, signs)) * root
    att_ref[0] = turned[0:STEPS].astype(BF16)
    att_ref[1] = turned[STEPS : 2 * STEPS].astype(BF16)
    att_copy = pltpu.make_async_copy(att_ref, att_hbm, small_sems.at[0])
    att_copy.start()

    sent = pltpu.make_async_remote_copy(
        src_ref=tbl.at[0], dst_ref=tbl.at[0], send_sem=far_send, recv_sem=far_recv,
        device_id={"batch": partner}, device_id_type=MESH,
    )
    pl.when(at_end)(sent.wait_send)
    att_copy.wait()

    loop(0, LAYERS, lambda at: out_copy(at).wait())
    rows_sent = send.at[pl.ds(0, SEQ - 1)]
    pltpu.make_async_remote_copy(
        src_ref=rows_sent, dst_ref=rows_sent, send_sem=a2a_send, recv_sem=far_recv,
        device_id={"seq": me}, device_id_type=MESH,
    ).wait_send()


def finish_kernel(app_hbm, got_hbm, att_hbm, out_hbm, app, in_sems, out_sems, att_sem):
    att_copy = pltpu.make_async_copy(got_hbm, att_hbm, att_sem)
    att_copy.start()
    chunks, rows = 4, SEQ * CAP // 4
    ins, outs = [], []
    for c in range(chunks):
        part = (slice(None), pl.ds(c * rows, rows))
        ins.append(pltpu.make_async_copy(app_hbm.at[part], app.at[part], in_sems.at[c]))
        outs.append(pltpu.make_async_copy(app.at[part], out_hbm.at[part], out_sems.at[c]))
    for copy in ins:
        copy.start()
    for into, out in zip(ins, outs):
        into.wait()
        out.start()
    for copy in outs:
        copy.wait()
    att_copy.wait()


def local(queries, cache_levels, scale_ids, scale_table, ctx_len, span_rows, span_len, owners):
    anywhere = pl.BlockSpec(memory_space=pl.ANY)
    dma = pltpu.SemaphoreType.DMA
    turn = lambda x: jnp.swapaxes(x, -1, -2)
    appended, attended = pl.pallas_call(
        exchange_kernel,
        out_shape=(
            jax.ShapeDtypeStruct((REQ, SEQ * CAP, WIDTH), BF16),
            jax.ShapeDtypeStruct((REQ, STEPS, HD), BF16),
        ),
        in_specs=[anywhere] * 8,
        out_specs=(anywhere, anywhere),
        scratch_shapes=[
            pltpu.VMEM((SEQ, 16, PIECE), BF16),
            pltpu.VMEM((REQ, SEQ * CAP, WIDTH), BF16),
            pltpu.SMEM((REQ, SLOT // GROUP), jnp.int32),
            pltpu.SMEM((1, REQ), jnp.int32),
            pltpu.SMEM((1, REQ), jnp.int32),
            pltpu.VMEM((REQ, 1, SPAN), jnp.int32),
            pltpu.VMEM((REQ, STEPS, HD), BF16),
            pltpu.VMEM((REQ, STEPS, HQ * HD), BF16),
            pltpu.VMEM((REQ, SLOT, WIDTH), BF16),
            pltpu.VMEM((REQ, SPAN, WIDTH), BF16),
            pltpu.VMEM((SEQ, 16, PIECE), BF16),
            pltpu.VMEM((2, BATCH_Y, NSCALE, 256), F32),
            pltpu.VMEM((2, BATCH_Y, REQ * (SLOT // GROUP), 256), F32),
            pltpu.VMEM((HQ * 8, HD), BF16),
            pltpu.VMEM((64, REQ * (SLOT + SPAN)), F32),
            pltpu.VMEM((PLANE, 64, HD), F32),
            pltpu.VMEM((PLANE, 64, HD), F32),
            pltpu.VMEM((PLANE, 2, HD), F32),
            pltpu.VMEM((PLANE, 2, HD), F32),
            pltpu.VMEM((LAYERS, 8, HD), F32),
            pltpu.VMEM((LAYERS, 8, HD), F32),
            pltpu.VMEM((1, 2, HD), F32),
            pltpu.VMEM((LAYERS, 2, HD), F32),
        ]
        + [dma((4,))]
        + [dma] * 4
        + [dma((LAYERS,)), dma, dma((LAYERS,))]
        + [dma] * 14
        + [pltpu.SemaphoreType.REGULAR((LAYERS,)), pltpu.SemaphoreType.REGULAR],
        compiler_params=pltpu.CompilerParams(
            collective_id=0, has_side_effects=True, vmem_limit_bytes=VMEM
        ),
        cost_estimate=pl.CostEstimate(
            flops=2 * 10**9, bytes_accessed=5 * 2**20, transcendentals=400000
        ),
        name="exchange",
    )(
        queries, cache_levels, scale_ids, scale_table,
        turn(ctx_len), span_rows, turn(span_len), turn(owners),
    )
    return pl.pallas_call(
        finish_kernel,
        out_shape=(
            jax.ShapeDtypeStruct((REQ, STEPS, HD), BF16),
            jax.ShapeDtypeStruct((REQ, SEQ * CAP, WIDTH), BF16),
        ),
        in_specs=[anywhere, anywhere],
        out_specs=(anywhere, anywhere),
        scratch_shapes=[
            pltpu.VMEM((REQ, SEQ * CAP, WIDTH), BF16),
            dma((4,)),
            dma((4,)),
            dma,
        ],
        compiler_params=pltpu.CompilerParams(vmem_limit_bytes=VMEM),
        name="finish",
    )(appended, attended)


def solution(mesh):
    return jax.shard_map(
        local,
        mesh=mesh,
        in_specs=(
            P("batch", None, None),
            P("batch", "seq", None),
            P("batch", "seq"),
            P(None, "batch"),
            P("batch", "seq"),
            P("batch", "seq", None),
            P("batch", "seq"),
            P("batch", "seq", None),
        ),
        out_specs=(P("batch", None, "seq"), P("batch", "seq", None)),
        check_vma=False,
    )
```

```python
import functools

import jax
import jax.numpy as jnp
from jax import lax
from jax.experimental import pallas as pl
from jax.experimental.pallas import tpu as pltpu
from jax.sharding import PartitionSpec as P

HQ = 64
KVH = 8
HD = 128
G = 8
CAP = 2
GROUP = 32
NSCALE = 16
STEPS = 4
SLOT = 256
SPAN = 64
REQ = 2
WIDTH = 2 * KVH * HD
SEQ = 64
PLANE = 8
LAYERS = 8
BATCH_Y = 4
PIECE = WIDTH // 4
VMEM = 60 * 2**20
MESH = pl.DeviceIdType.MESH
F32 = jnp.float32
BF16 = jnp.bfloat16


def iota(shape, axis):
    return lax.broadcasted_iota(jnp.int32, shape, axis)


def hadamard_signs():
    common = jnp.bitwise_and(iota((HD, HD), 0), iota((HD, HD), 1))
    parity = jnp.zeros((HD, HD), jnp.int32)
    for bit in range(7):
        parity = parity + jnp.bitwise_and(jnp.right_shift(common, bit), 1)
    return (1 - 2 * jnp.bitwise_and(parity, 1)).astype(F32).astype(BF16)


def dot(a, b, contract=((1,), (0,))):
    return lax.dot_general(a, b, (contract, ((), ())), preferred_element_type=F32)


def as_column(row, hot):
    return jnp.sum(jnp.where(hot, jnp.broadcast_to(row, hot.shape), 0.0), axis=1, keepdims=True)


def join(stats):
    tops = jnp.concatenate([stat[0:1] for stat in stats], axis=0)
    totals = jnp.concatenate([stat[1:2] for stat in stats], axis=0)
    top = jnp.max(tops, axis=0, keepdims=True)
    factors = jnp.exp(tops - top)
    return factors, top, jnp.sum(totals * factors, axis=0, keepdims=True)


def exchange_kernel(
    q_hbm, lev_hbm, ids_hbm, tab_hbm, ctx_hbm, span_hbm, slen_hbm, own_hbm,
    app_hbm, att_hbm,
    land, app, ids_ref, ctx_ref, slen_ref, own_ref, att_ref,
    q_ref, lev, span, send, tbl, scales, qrot, mask,
    first_out, first_in, first_stat, first_got, second_out, second_in, second_stat, second_got,
    small_sems, q_sem, tab_sem, lev_sem, span_sem, app_sems,
    a2a_send, a2a_recv, far_send, far_recv, near_send, near_recv, side_send, side_recv,
    first_send, first_recv, first_stat_send, first_stat_recv,
    second_send, second_recv, second_stat_send, second_stat_recv,
    ready, joined,
):
    me = lax.axis_index("seq")
    layer, place = me // PLANE, lax.rem(me, PLANE)
    batch = lax.axis_index("batch")
    far, row = batch // BATCH_Y, lax.rem(batch, BATCH_Y)
    partner = lax.rem(batch + BATCH_Y, 2 * BATCH_Y)
    sides = [far * BATCH_Y + lax.rem(row + i, BATCH_Y) for i in range(1, BATCH_Y)]
    lower = layer < LAYERS // 2

    def loop(start, stop, body):
        def step(i, carry):
            body(i)
            return carry

        lax.fori_loop(start, stop, step, 0)

    barrier = pltpu.get_barrier_semaphore()

    def greet(to):
        pl.semaphore_signal(barrier, inc=1, device_id=to, device_id_type=MESH)

    loop(1, PLANE, lambda i: greet({"seq": layer * PLANE + lax.rem(place + i, PLANE)}))
    for side in sides:
        greet({"batch": side})

    at_end = (layer == 0) | (layer == LAYERS - 1)
    sender = {"seq": jnp.where(lower, LAYERS - 1, 0) * PLANE + place, "batch": partner}

    def taker(i):
        return {
            "seq": (jnp.where(layer == 0, LAYERS // 2, 0) + i) * PLANE + place,
            "batch": partner,
        }

    @pl.when(far == 0)
    def _():
        greet(sender)
        pl.when(at_end)(lambda: loop(0, LAYERS // 2, lambda i: greet(taker(i))))

    loop((layer + 1) * PLANE, SEQ, lambda i: greet({"seq": i}))
    pl.when(far == 1)(lambda: loop(0, layer * PLANE, lambda i: greet({"seq": i})))

    small = [
        pltpu.make_async_copy(here, there, small_sems.at[i])
        for i, (here, there) in enumerate(
            ((own_hbm, own_ref), (slen_hbm, slen_ref), (ctx_hbm, ctx_ref), (ids_hbm, ids_ref))
        )
    ]
    for copy in small:
        copy.start()
    span_copy = pltpu.make_async_copy(span_hbm, span, span_sem)
    span_copy.start()
    tab_copy = pltpu.make_async_copy(tab_hbm, tbl.at[far, row], tab_sem)
    tab_copy.start()
    q_copy = pltpu.make_async_copy(q_hbm, q_ref, q_sem)
    q_copy.start()
    lev_copy = pltpu.make_async_copy(lev_hbm, lev, lev_sem)
    lev_copy.start()

    for copy in small:
        copy.wait()
    owner_row = jnp.concatenate([own_ref[0], own_ref[1]], axis=1).astype(F32)
    above, along = iota((2 * SPAN, 2 * SPAN), 0), iota((2 * SPAN, 2 * SPAN), 1)
    owner_wide = jnp.broadcast_to(owner_row, (2 * SPAN, 2 * SPAN))
    owner_col = jnp.sum(jnp.where(above == along, owner_wide, 0.0), axis=1, keepdims=True)
    same = (owner_wide == owner_col) & (above < along) & (above // SPAN == along // SPAN)
    rank = jnp.sum(jnp.where(same, 1.0, 0.0), axis=0, keepdims=True)
    lane = iota((1, 2 * SPAN), 1)
    request = lane // SPAN
    kept = lax.rem(lane, SPAN) < jnp.where(request == 0, slen_ref[0, 0], slen_ref[0, 1])
    target = owner_row.astype(jnp.int32) * 16 + request * 8 + rank.astype(jnp.int32)
    target = jnp.concatenate(
        [jnp.where(kept, target + 2 * quarter, -1) for quarter in range(4)], axis=1
    )
    span_copy.wait()
    stacked = jnp.concatenate(
        [
            span[r, :, quarter * PIECE : (quarter + 1) * PIECE]
            for quarter in range(4)
            for r in range(REQ)
        ],
        axis=0,
    )
    for to_layer in range(LAYERS):
        rows = iota((16 * PLANE, REQ * SPAN * 4), 0) + to_layer * (16 * PLANE)
        pick = jnp.where(rows == target, 1.0, 0.0).astype(BF16)
        block = dot(pick, stacked).astype(BF16)
        send[pl.ds(to_layer * PLANE, PLANE)] = block.reshape(PLANE, 16, PIECE)

    known = far * (1 + jnp.where(at_end, LAYERS // 2, 0))
    layers_known = jnp.where(far == 0, layer, LAYERS - 1)
    pl.semaphore_wait(barrier, PLANE - 1 + BATCH_Y - 1 + layers_known * PLANE + known)

    loop(
        0,
        jnp.where(far == 0, layer, 0),
        lambda i: pl.semaphore_signal(
            ready.at[layer], inc=1, device_id={"seq": i * PLANE + place}, device_id_type=MESH
        ),
    )

    tab_copy.wait()
    def to_other_half():
        def one(i):
            pltpu.make_async_remote_copy(
                src_ref=tbl.at[far, row], dst_ref=tbl.at[far, row],
                send_sem=far_send, recv_sem=far_recv, device_id=taker(i), device_id_type=MESH,
            ).start()

        loop(0, LAYERS // 2, one)

    @pl.when(far == 1)
    def _():
        pl.when(at_end)(to_other_half)
        pl.semaphore_signal(joined, inc=1, device_id=sender, device_id_type=MESH)

    def to_sides(half, send_sem, recv_sem):
        for side in sides:
            pltpu.make_async_remote_copy(
                src_ref=tbl.at[half, row], dst_ref=tbl.at[half, row],
                send_sem=send_sem, recv_sem=recv_sem,
                device_id={"batch": side}, device_id_type=MESH,
            ).start()

    def from_sides(send_sem, recv_sem):
        some = tbl.at[0, pl.ds(0, BATCH_Y - 1)]
        every = pltpu.make_async_remote_copy(
            src_ref=some, dst_ref=some, send_sem=send_sem, recv_sem=recv_sem,
            device_id={"batch": partner}, device_id_type=MESH,
        )
        every.wait_send()
        every.wait_recv()

    to_sides(far, near_send, near_recv)

    def await_layer(to_layer):
        pl.when((to_layer > layer) & (far == 0))(lambda: pl.semaphore_wait(ready.at[to_layer], 1))

    def send_rows(to_layer, start=0):
        def one(i):
            to = to_layer * PLANE + lax.rem(place + i, PLANE)
            pltpu.make_async_remote_copy(
                src_ref=send.at[to], dst_ref=land.at[me], send_sem=a2a_send, recv_sem=a2a_recv.at[layer],
                device_id={"seq": to}, device_id_type=MESH,
            ).start()

        loop(start, PLANE, one)

    def post(to_layer):
        await_layer(to_layer)
        send_rows(to_layer)

    half = LAYERS // 2
    own = jnp.where(lower, layer, LAYERS - 1 - layer)

    def counted(number):
        return jnp.where(lower, number, LAYERS - 1 - number)

    across = [
        jnp.where(lower, half + up, half - 1 - jnp.where(far == 0, down, other))
        for up, down, other in zip((0, 3, 2, 1), (3, 2, 1, 0), (0, 3, 2, 1))
    ]

    def post_inner():
        for number in range(half - 1, 0, -1):
            pl.when(number > own)(functools.partial(post, counted(number)))

    def each_outer(act):
        for number in range(half - 2, -1, -1):
            pl.when(number < own)(functools.partial(act, counted(number)))

    def post_some(layers):
        for to_layer in layers:
            post(to_layer)

    post_inner()
    hold = (own < 2) & (far == 0)
    post_some(across[:2])
    pl.when(jnp.logical_not(hold))(lambda: post(across[2]))
    send_rows(layer, 1)
    each_outer(post)
    land[me] = send[me]

    @pl.when((far == 0) & at_end)
    def _():
        pl.semaphore_wait(joined, LAYERS // 2)
        to_other_half()

    signs = hadamard_signs()
    root = jnp.float32(1.0) / jnp.sqrt(jnp.float32(HD))
    q_copy.wait()
    queries = jnp.concatenate([q_ref[0].astype(F32), q_ref[1].astype(F32)], axis=0)
    stacked_q = jnp.concatenate(
        [queries[:, h * HD : (h + 1) * HD] for h in range(HQ)], axis=0
    ).astype(BF16)
    qrot[...] = (dot(stacked_q, signs) * root).astype(BF16)

    keys = REQ * (SLOT + SPAN)
    wanted = lax.rem(iota((64, keys), 0) // STEPS, REQ)
    column = iota((64, keys), 1)
    in_slot = column < REQ * SLOT
    other = column - REQ * SLOT
    key_request = jnp.where(in_slot, column // SLOT, other // SPAN)
    position = jnp.where(in_slot, lax.rem(column, SLOT), lax.rem(other, SPAN))
    first = key_request == 0
    limit = jnp.where(
        in_slot,
        jnp.where(first, ctx_ref[0, 0], ctx_ref[0, 1]),
        jnp.where(first, slen_ref[0, 0], slen_ref[0, 1]),
    )
    mask[...] = jnp.where((wanted == key_request) & (position < limit), 1.0, 0.0)
    blocks = REQ * (SLOT // GROUP)
    group = jnp.zeros((blocks, 3 * NSCALE), jnp.int32)
    for r in range(REQ):
        for b in range(SLOT // GROUP):
            here = iota((blocks, 3 * NSCALE), 0) == r * (SLOT // GROUP) + b
            group = jnp.where(here, ids_ref[r, b], group)
    chosen = jnp.where(lax.rem(iota((blocks, 3 * NSCALE), 1), NSCALE) == group, 1.0, 0.0).astype(BF16)

    pltpu.make_async_remote_copy(
        src_ref=tbl.at[0, 0], dst_ref=tbl.at[0, 0], send_sem=far_send, recv_sem=far_recv,
        device_id={"batch": partner}, device_id_type=MESH,
    ).wait_recv()
    to_sides(1 - far, side_send, side_recv)
    from_sides(near_send, near_recv)
    from_sides(side_send, side_recv)

    for f in range(2):
        for r in range(BATCH_Y):
            piece = tbl[f, r]
            high = piece.astype(BF16)
            remain = piece - high.astype(F32)
            middle = remain.astype(BF16)
            low = (remain - middle.astype(F32)).astype(BF16)
            scales[f, r] = dot(chosen, jnp.concatenate([high, middle, low], axis=0))
    lev_copy.wait()

    lane = iota((64, HD), 1)
    sub = lax.rem(iota((64, HD), 0), 8)

    def dequant(pair, half, base, part):
        pieces = []
        lanes = pl.ds(pl.multiple_of(base, HD), HD)
        for r in range(REQ):
            for b in range(SLOT // GROUP):
                at = r * (SLOT // GROUP) + b
                scale = scales[part, pair, at : at + 1, half * HD : (half + 1) * HD]
                level = lev[r, b * GROUP : (b + 1) * GROUP, lanes].astype(F32)
                pieces.append((level * scale).astype(BF16))
        for r in range(REQ):
            pieces.append(span[r, :, lanes])
        return jnp.concatenate(pieces, axis=0)

    def head_pair(pair, carry):
        tops, totals = carry
        for half in range(2):
            head = pair * 2 + half
            key_rows = dequant(pair, half, head * HD, 0)
            q = qrot[pl.ds(pl.multiple_of(head * 64, 64), 64), :]
            scores = dot(q, key_rows, ((1,), (1,))) * root
            scores = jnp.where(mask[...] > 0.0, scores, jnp.float32(-1e30))
            top = jnp.max(scores, axis=1, keepdims=True)
            weights = jnp.exp(scores - top)
            total = jnp.sum(weights, axis=1, keepdims=True)
            value_rows = dequant(pair, half, (KVH + head) * HD, 1)
            acc = dot(weights.astype(BF16), value_rows)
            hot = lane == head * 8 + sub
            tops = tops + jnp.sum(jnp.where(hot, top, 0.0).reshape(G, 8, HD), axis=1)
            totals = totals + jnp.sum(jnp.where(hot, total, 0.0).reshape(G, 8, HD), axis=1)
            at = pl.ds(pl.multiple_of(head * 8, 8), 8)
            for g in range(G):
                first_out[g, at, :] = acc[g * 8 : (g + 1) * 8]
        return tops, totals

    zeros = jnp.zeros((G, HD), F32)
    tops, totals = lax.fori_loop(0, KVH // 2, head_pair, (zeros, zeros))
    for g in range(G):
        first_stat[g, 0:1] = tops[g : g + 1]
        first_stat[g, 1:2] = totals[g : g + 1]

    def first_post(i):
        to = lax.rem(place + i, PLANE)
        for out, into, send_sem, recv_sem in (
            (first_out, first_in, first_send, first_recv),
            (first_stat, first_got, first_stat_send, first_stat_recv),
        ):
            pltpu.make_async_remote_copy(
                src_ref=out.at[to], dst_ref=into.at[place], send_sem=send_sem, recv_sem=recv_sem,
                device_id={"seq": layer * PLANE + to}, device_id_type=MESH,
            ).start()

    def wait_all(out, into, count, send_sem, recv_sem):
        every = pltpu.make_async_remote_copy(
            src_ref=out.at[pl.ds(0, count)], dst_ref=into.at[pl.ds(0, count)],
            send_sem=send_sem, recv_sem=recv_sem, device_id={"seq": me}, device_id_type=MESH,
        )
        every.wait_send()
        every.wait_recv()

    loop(1, PLANE, first_post)
    first_in[place] = first_out[place]
    first_got[place] = first_stat[place]
    wait_all(first_out, first_in, PLANE - 1, first_send, first_recv)
    wait_all(first_stat, first_got, PLANE - 1, first_stat_send, first_stat_recv)
    factors, top, total = join([first_got[i] for i in range(PLANE)])
    hot = lane == iota((64, HD), 0)
    acc = None
    for i in range(PLANE):
        term = first_in[i] * as_column(factors[i : i + 1], hot)
        acc = term if acc is None else acc + term
    second_out[...] = acc.reshape(LAYERS, 8, HD)
    second_stat[0, 0:1] = top
    second_stat[0, 1:2] = total

    def second_post(i):
        to = lax.rem(layer + i, LAYERS)
        for out, into, send_sem, recv_sem in (
            (second_out.at[to], second_in, second_send, second_recv),
            (second_stat.at[0], second_got, second_stat_send, second_stat_recv),
        ):
            pltpu.make_async_remote_copy(
                src_ref=out, dst_ref=into.at[layer], send_sem=send_sem, recv_sem=recv_sem,
                device_id={"seq": to * PLANE + place}, device_id_type=MESH,
            ).start()

    pl.when(hold)(lambda: await_layer(across[2]))
    for to_layer in across[3 :]:
        await_layer(to_layer)
    loop(1, LAYERS, second_post)
    pl.when(hold)(lambda: send_rows(across[2]))
    for to_layer in across[3 :]:
        send_rows(to_layer)
    second_in[layer] = second_out[layer]
    second_got[layer] = second_stat[0]
    to = iota((128, 128), 0)
    request, quarter = to // 64, lax.rem(to // 16, 4)
    source, rank = lax.rem(to // 2, 8), lax.rem(to, 2)
    wanted = source * 16 + request * 8 + quarter * 2 + rank
    move = jnp.where(iota((128, 128), 1) == wanted, 1.0, 0.0).astype(BF16)

    def out_copy(at):
        rows = pl.ds(pl.multiple_of(at * 16, 16), 16)
        return pltpu.make_async_copy(app.at[:, rows, :], app_hbm.at[:, rows, :], app_sems.at[at])

    def place_layer(at, count):
        some = land.at[pl.ds(0, count)]
        pltpu.make_async_remote_copy(
            src_ref=some, dst_ref=some, send_sem=a2a_send, recv_sem=a2a_recv.at[at],
            device_id={"seq": me}, device_id_type=MESH,
        ).wait_recv()
        block = land[pl.ds(at * PLANE, PLANE)].reshape(128, PIECE)
        moved = dot(move, block).astype(BF16)
        rows = pl.ds(pl.multiple_of(at * 16, 16), 16)
        for r in range(REQ):
            for q in range(4):
                start = r * 64 + q * 16
                app[r, rows, q * PIECE : (q + 1) * PIECE] = moved[start : start + 16]
        out_copy(at).start()

    place_layer(layer, PLANE - 1)
    for i in range(1, half):
        place_layer(layer // half * half + lax.rem(layer + i, half), PLANE)
    for i in range(half):
        place_layer(counted(LAYERS - 1 - i), PLANE)
    wait_all(second_out, second_in, LAYERS - 1, second_send, second_recv)
    wait_all(second_got, second_got, LAYERS - 1, second_stat_send, second_stat_recv)
    factors, _, total = join([second_got[i] for i in range(LAYERS)])
    hot = iota((8, HD), 1) == layer * 8 + iota((8, HD), 0)
    acc = None
    for i in range(LAYERS):
        term = second_in[i] * as_column(factors[i : i + 1], hot)
        acc = term if acc is None else acc + term
    normed = acc / as_column(total, hot)
    high = normed.astype(BF16)
    remain = normed - high.astype(F32)
    middle = remain.astype(BF16)
    low = (remain - middle.astype(F32)).astype(BF16)
    turned = (dot(low, signs) + dot(middle, signs) + dot(high, signs)) * root
    att_ref[0] = turned[0:STEPS].astype(BF16)
    att_ref[1] = turned[STEPS : 2 * STEPS].astype(BF16)
    att_copy = pltpu.make_async_copy(att_ref, att_hbm, small_sems.at[0])
    att_copy.start()

    sent = pltpu.make_async_remote_copy(
        src_ref=tbl.at[0], dst_ref=tbl.at[0], send_sem=far_send, recv_sem=far_recv,
        device_id={"batch": partner}, device_id_type=MESH,
    )
    pl.when(at_end)(sent.wait_send)
    att_copy.wait()

    loop(0, LAYERS, lambda at: out_copy(at).wait())
    rows_sent = send.at[pl.ds(0, SEQ - 1)]
    pltpu.make_async_remote_copy(
        src_ref=rows_sent, dst_ref=rows_sent, send_sem=a2a_send, recv_sem=far_recv,
        device_id={"seq": me}, device_id_type=MESH,
    ).wait_send()


def finish_kernel(app_hbm, got_hbm, att_hbm, out_hbm, app, in_sems, out_sems, att_sem):
    att_copy = pltpu.make_async_copy(got_hbm, att_hbm, att_sem)
    att_copy.start()
    chunks, rows = 4, SEQ * CAP // 4
    ins, outs = [], []
    for c in range(chunks):
        part = (slice(None), pl.ds(c * rows, rows))
        ins.append(pltpu.make_async_copy(app_hbm.at[part], app.at[part], in_sems.at[c]))
        outs.append(pltpu.make_async_copy(app.at[part], out_hbm.at[part], out_sems.at[c]))
    for copy in ins:
        copy.start()
    for into, out in zip(ins, outs):
        into.wait()
        out.start()
    for copy in outs:
        copy.wait()
    att_copy.wait()


def local(queries, cache_levels, scale_ids, scale_table, ctx_len, span_rows, span_len, owners):
    anywhere = pl.BlockSpec(memory_space=pl.ANY)
    dma = pltpu.SemaphoreType.DMA
    turn = lambda x: jnp.swapaxes(x, -1, -2)
    appended, attended = pl.pallas_call(
        exchange_kernel,
        out_shape=(
            jax.ShapeDtypeStruct((REQ, SEQ * CAP, WIDTH), BF16),
            jax.ShapeDtypeStruct((REQ, STEPS, HD), BF16),
        ),
        in_specs=[anywhere] * 8,
        out_specs=(anywhere, anywhere),
        scratch_shapes=[
            pltpu.VMEM((SEQ, 16, PIECE), BF16),
            pltpu.VMEM((REQ, SEQ * CAP, WIDTH), BF16),
            pltpu.SMEM((REQ, SLOT // GROUP), jnp.int32),
            pltpu.SMEM((1, REQ), jnp.int32),
            pltpu.SMEM((1, REQ), jnp.int32),
            pltpu.VMEM((REQ, 1, SPAN), jnp.int32),
            pltpu.VMEM((REQ, STEPS, HD), BF16),
            pltpu.VMEM((REQ, STEPS, HQ * HD), BF16),
            pltpu.VMEM((REQ, SLOT, WIDTH), BF16),
            pltpu.VMEM((REQ, SPAN, WIDTH), BF16),
            pltpu.VMEM((SEQ, 16, PIECE), BF16),
            pltpu.VMEM((2, BATCH_Y, NSCALE, 256), F32),
            pltpu.VMEM((2, BATCH_Y, REQ * (SLOT // GROUP), 256), F32),
            pltpu.VMEM((HQ * 8, HD), BF16),
            pltpu.VMEM((64, REQ * (SLOT + SPAN)), F32),
            pltpu.VMEM((PLANE, 64, HD), F32),
            pltpu.VMEM((PLANE, 64, HD), F32),
            pltpu.VMEM((PLANE, 2, HD), F32),
            pltpu.VMEM((PLANE, 2, HD), F32),
            pltpu.VMEM((LAYERS, 8, HD), F32),
            pltpu.VMEM((LAYERS, 8, HD), F32),
            pltpu.VMEM((1, 2, HD), F32),
            pltpu.VMEM((LAYERS, 2, HD), F32),
        ]
        + [dma((4,))]
        + [dma] * 4
        + [dma((LAYERS,)), dma, dma((LAYERS,))]
        + [dma] * 14
        + [pltpu.SemaphoreType.REGULAR((LAYERS,)), pltpu.SemaphoreType.REGULAR],
        compiler_params=pltpu.CompilerParams(
            collective_id=0, has_side_effects=True, vmem_limit_bytes=VMEM
        ),
        cost_estimate=pl.CostEstimate(
            flops=2 * 10**9, bytes_accessed=5 * 2**20, transcendentals=400000
        ),
        name="exchange",
    )(
        queries, cache_levels, scale_ids, scale_table,
        turn(ctx_len), span_rows, turn(span_len), turn(owners),
    )
    return pl.pallas_call(
        finish_kernel,
        out_shape=(
            jax.ShapeDtypeStruct((REQ, STEPS, HD), BF16),
            jax.ShapeDtypeStruct((REQ, SEQ * CAP, WIDTH), BF16),
        ),
        in_specs=[anywhere, anywhere],
        out_specs=(anywhere, anywhere),
        scratch_shapes=[
            pltpu.VMEM((REQ, SEQ * CAP, WIDTH), BF16),
            dma((4,)),
            dma((4,)),
            dma,
        ],
        compiler_params=pltpu.CompilerParams(vmem_limit_bytes=VMEM),
        name="finish",
    )(appended, attended)


def solution(mesh):
    return jax.shard_map(
        local,
        mesh=mesh,
        in_specs=(
            P("batch", None, None),
            P("batch", "seq", None),
            P("batch", "seq"),
            P(None, "batch"),
            P("batch", "seq"),
            P("batch", "seq", None),
            P("batch", "seq"),
            P("batch", "seq", None),
        ),
        out_specs=(P("batch", None, "seq"), P("batch", "seq", None)),
        check_vma=False,
    )
```
